256 devices in a mesh: cuts: 16 (over y_hi, z), tile: 16 (over x, y_lo, core).
Axes of the slice: x: 4, y: 4 (y_hi: 2, y_lo: 2; y = y_hi * 2 + y_lo), z: 8, core: 2. Of those that a mesh axis runs over, the one named last changes fastest.
Arguments:
- field_in: float32 [384, 2, 256, 384], P('tile', None, 'cuts'), may hold values from -6 to 6
- propagator: bfloat16 [2, 384, 384], replicated
- theta: float32 [256, 32768], P('cuts', 'tile'), may hold values from -3.140625 to 3.140625
- cell_x: int32 [256, 2, 32768], P('cuts', None, 'tile'), may hold values from 0 to 23
- cell_y: int32 [256, 2, 32768], P('cuts', None, 'tile'), may hold values from 0 to 383
- src_dev: int32 [256, 2], replicated, may hold values from 0 to 15, all different within a row; in each aligned block of 16 rows (0 to 15, 16 to 31, ...) at most 4 rows name the same one
- src_slot: int32 [256, 2], replicated, may hold values from 0 to 15
- weights: float32 [256, 2], replicated, may hold values from 0.5 to 1.5
- coupling: float32 [2, 2], replicated, may hold values from 0.4 to 1.2
Outputs:
- field_out: float32 [384, 2, 256, 384], P('tile', None, 'cuts')
The draws below stay inside these ranges and needn't reach their ends.
Inputs may be any that keep to these rules, and one draw needn't show every extreme that they name: `src_dev`: each row names 2 different values; in each aligned block of 16 rows no value is named by more than 4 rows.
All inputs are finite; a program needn't handle non-finite values.
Results may differ from the reference program's by a relative error of at most 0.0052.
Values may be sent and summed in bfloat16 or wider, within the bound.
A program may use at most 64 MiB of HBM per device.

```python
import math
from functools import partial
import jax
import jax.numpy as jnp
import numpy as np
from jax import lax

GRID = 384
S_DEV = 16
MT = 2048
K = 2
HARM = 5
PERIODS = 2
SLICES = 256
X_DEV = 24
PART = 32768
CAP = 4
N_CUTS = 16
N_TILE = 16


def draw_propagator(key, part):
    noise_key = jax.random.fold_in(key, 11)
    diagonal = (jnp.arange(GRID)[:, None] == jnp.arange(GRID)[None, :]).astype(jnp.float32)
    noise = jax.random.normal(noise_key, (2, GRID, GRID), jnp.float32) * (0.5 / math.sqrt(GRID))
    centre = jnp.stack([0.6 * diagonal, 0.3 * diagonal])
    return (centre + noise).astype(jnp.bfloat16)


def touch_ends(entries, own_key, smallest, largest):
    dims = entries.shape
    index_at = [jax.random.randint(jax.random.fold_in(own_key, axis), (), 0, dims[axis]) for axis in range(len(dims))]
    entries = entries.at[tuple(index_at)].set(smallest)
    longest = dims.index(max(dims))
    index_at[longest] = (index_at[longest] + 1) % dims[longest]
    return entries.at[tuple(index_at)].set(largest)


def level_of(key, extent, shards, low, largest):
    def one(axis_at, parts):
        steps = jax.random.uniform(jax.random.fold_in(jax.random.fold_in(key, 6), axis_at), (parts,), jnp.float32, low / len(shards), largest / len(shards))
        return jnp.repeat(jnp.exp(steps), extent[axis_at] // parts).reshape((-1,) + (1,) * (len(extent) - axis_at - 1))

    gain = one(*shards[0])
    for cut in shards[1:]:
        gain = gain * one(*cut)
    return gain


def assign_block(own_key, own, number, rows, number_of, top, reach, slope):
    order = jax.random.permutation(own_key, number_of)
    packed, common = load_shares(number_of, rows * top, reach, slope, True), load_shares(number_of, rows * top, reach, slope, False)
    places = jnp.arange(number_of)

    def named(tallies, turn):
        used = int((tallies > 0).sum())
        fixed = max(1, used // 4)
        passed = fixed + (places - fixed + turn * (used - fixed)) % max(1, number_of - fixed)
        return jnp.zeros((number_of,), jnp.int32).at[order[jnp.where(places < fixed, places, passed)]].set(jnp.asarray(tallies, jnp.int32))

    tallies = jnp.where(number % 4 == 0, named(packed, number // 4), named(common, number - number // 4 - 1))
    mixed = jax.random.permutation(jax.random.fold_in(own, 3), number_of)
    source_of, receiver = mixed[0:number_of // 2 * 2:2], mixed[1:number_of // 2 * 2:2]
    slack = jnp.minimum(tallies[source_of] - 1, reach - tallies[receiver]) // 2
    slack = jnp.where((source_of == order[0]) | (receiver == order[0]) | (tallies[receiver] == 0), 0, jnp.maximum(slack, 0))
    passed = jax.random.randint(jax.random.fold_in(own, 4), (number_of // 2,), 0, 1 << 20) % (slack + 1)
    tallies = tallies.at[source_of].add(-passed).at[receiver].add(passed)
    labels = jnp.searchsorted(jnp.cumsum(tallies), jnp.arange(rows * top), side="right").astype(jnp.int32)
    listing = labels.reshape(top, rows).T
    listing = listing[jax.random.permutation(jax.random.fold_in(own, 1), rows)]
    turn = jax.random.randint(jax.random.fold_in(own, 2), (rows, 1), 0, top)
    return jnp.take_along_axis(listing, (jnp.arange(top)[None, :] + turn) % top, axis=1)


def load_shares(count, total, bound, slope, full):
    weights = [(1 << 20) // math.isqrt(rank ** slope) + 1 for rank in range(1, count + 1)]
    largest = bound if full else min(bound, max(-(-total // count), total * weights[0] // sum(weights)))
    least = 1 if total - largest >= count - 1 else 0
    given, rest = [largest] + [least] * (count - 1), total - largest - least * (count - 1)
    while rest > 0:
        movable = [i for i in range(1, count) if given[i] < largest] or [i for i in range(1, count) if given[i] < bound]
        pool, budget = sum([weights[i] for i in movable]), rest
        for i in movable:
            extra = min(bound - given[i], max(1, budget * weights[i] // pool), rest)
            given[i] = given[i] + extra
            rest = rest - extra
    return np.array(given)


def normal_values(stream_key, shape, deviation, bound, split=(), dtype=jnp.bfloat16):
    array = deviation * jax.random.normal(stream_key, shape, jnp.float32)
    if split:
        array = array * level_of(stream_key, shape, split, -0.22, 0.18)
    return jnp.clip(array, -bound, bound).astype(dtype)


def setup_inputs(seed: int = 0) -> dict:
    keys = jax.random.split(jax.random.key(seed), 10)
    field_in = normal_values(keys[0], (GRID, 2, SLICES, GRID), 1.0, 6.0, ((0, 16), (2, 16)), jnp.float32)
    propagator = draw_propagator(jax.random.fold_in(keys[9], 71), 0)
    theta = jnp.clip(jax.random.uniform(keys[2], (SLICES, PART), jnp.float32, -3.140625, 3.140625), -3.140625, 3.140625)
    cell_x = touch_ends(jax.random.randint(keys[3], (SLICES, K, PART), 0, X_DEV), jax.random.fold_in(keys[3], 1), 0, X_DEV - 1).astype(jnp.int32)
    cell_y = touch_ends(jax.random.randint(keys[4], (SLICES, K, PART), 0, GRID), jax.random.fold_in(keys[4], 1), 0, GRID - 1).astype(jnp.int32)
    src_dev_keys = jax.random.split(jax.random.fold_in(keys[5], 1), SLICES // S_DEV)
    src_dev_turns = jax.random.permutation(jax.random.fold_in(keys[5], 3), SLICES // S_DEV)
    src_dev = jax.vmap(lambda own, number: assign_block(jax.random.fold_in(keys[5], 2), own, number, S_DEV, N_CUTS, K, CAP, 2))(src_dev_keys, src_dev_turns).reshape((SLICES, K))
    src_slot = touch_ends(jax.random.randint(keys[6], (SLICES, K), 0, S_DEV), jax.random.fold_in(keys[6], 1), 0, S_DEV - 1).astype(jnp.int32)
    weights = jnp.clip(jax.random.uniform(keys[7], (SLICES, K), jnp.float32, 0.5, 1.5), 0.5, 1.5)
    coupling = jnp.clip(jax.random.uniform(keys[8], (PERIODS, 2), jnp.float32, 0.4, 1.2), 0.4, 1.2)
    return {"field_in": field_in, "propagator": propagator, "theta": theta, "cell_x": cell_x, "cell_y": cell_y, "src_dev": src_dev, "src_slot": src_slot, "weights": weights, "coupling": coupling}


def deposit_slice(theta, tile_rows, members):
    source_index, entry_weight, rows_x, cols_y = members
    phases = jnp.take(theta, source_index, axis=0)
    angle = HARM * phases
    real_part = (entry_weight[:, None] * jnp.cos(angle)).astype(jnp.bfloat16)
    imag_part = (entry_weight[:, None] * jnp.sin(angle)).astype(jnp.bfloat16)
    real_part, imag_part = lax.optimization_barrier((real_part, imag_part))
    cell_index = (cols_y * GRID + rows_x + tile_rows[None, :]).astype(jnp.int32).reshape(-1)
    flat_real = jnp.zeros((GRID * GRID,), jnp.float32).at[cell_index].add(real_part.astype(jnp.float32).reshape(-1))
    flat_imag = jnp.zeros((GRID * GRID,), jnp.float32).at[cell_index].add(imag_part.astype(jnp.float32).reshape(-1))
    return jnp.stack([flat_real, flat_imag], -1).reshape(GRID, GRID, 2).astype(jnp.bfloat16)


def along_y(prop_real, prop_imag, field_real, field_imag):
    real_part = jnp.dot(prop_real, field_real, preferred_element_type=jnp.float32) - jnp.dot(prop_imag, field_imag, preferred_element_type=jnp.float32)
    imag_part = jnp.dot(prop_real, field_imag, preferred_element_type=jnp.float32) + jnp.dot(prop_imag, field_real, preferred_element_type=jnp.float32)
    return real_part, imag_part


def along_x(prop_real, prop_imag, field_real, field_imag):
    real_part = jnp.dot(field_real, prop_real.T, preferred_element_type=jnp.float32) - jnp.dot(field_imag, prop_imag.T, preferred_element_type=jnp.float32)
    imag_part = jnp.dot(field_imag, prop_real.T, preferred_element_type=jnp.float32) + jnp.dot(field_real, prop_imag.T, preferred_element_type=jnp.float32)
    return real_part, imag_part


def period_slice(propagator, coupling_row, y_first, members):
    radiation, source = members
    src_real = source[..., 0].astype(jnp.float32)
    src_imag = source[..., 1].astype(jnp.float32)
    field_real = radiation[..., 0] + coupling_row[0] * src_real - coupling_row[1] * src_imag
    field_imag = radiation[..., 1] + coupling_row[0] * src_imag + coupling_row[1] * src_real
    round_real = field_real.astype(jnp.bfloat16)
    round_imag = field_imag.astype(jnp.bfloat16)
    prop_real = propagator[0]
    prop_imag = propagator[1]
    if y_first:
        inter_real, inter_imag = along_y(prop_real, prop_imag, round_real, round_imag)
        out_real, out_imag = along_x(prop_real, prop_imag, inter_real.astype(jnp.bfloat16), inter_imag.astype(jnp.bfloat16))
    else:
        inter_real, inter_imag = along_x(prop_real, prop_imag, round_real, round_imag)
        out_real, out_imag = along_y(prop_real, prop_imag, inter_real.astype(jnp.bfloat16), inter_imag.astype(jnp.bfloat16))
    return jnp.stack([out_real, out_imag], -1)


def reference(field_in, propagator, theta, cell_x, cell_y, src_dev, src_slot, weights, coupling):
    tile_rows = ((jnp.arange(PART) // MT) * (GRID // N_TILE)).astype(jnp.int32)
    source_index = (src_dev * S_DEV + src_slot).astype(jnp.int32)
    source = lax.map(partial(deposit_slice, theta, tile_rows), (source_index, weights, cell_x, cell_y))
    radiation = jnp.transpose(field_in, (2, 3, 0, 1))
    for period in range(PERIODS):
        radiation = lax.map(partial(period_slice, propagator, coupling[period], period % 2 == 0), (radiation, source))
        radiation = jnp.roll(radiation, 1, axis=0)
    return jnp.transpose(radiation, (2, 3, 0, 1))
```

```python
import functools
import math

import jax
import jax.numpy as jnp
from jax import lax
from jax.experimental import pallas as pl
from jax.experimental.pallas import tpu as pltpu
from jax.sharding import PartitionSpec as P

HARM = 5
CAP = 4
LANES = 128
MESH = pl.DeviceIdType.MESH
SIN_PI = (
    3.141592502593994,
    -5.1677069664001465,
    2.5500311851501465,
    -0.5980440974235535,
    0.07721816748380661,
)
F32 = jnp.float32
BF16 = jnp.bfloat16


def sin_pi(fraction):
    square = fraction * fraction
    total = jnp.full_like(square, SIN_PI[4])
    for coefficient in SIN_PI[3::-1]:
        total = total * square + coefficient
    return total * fraction


def dot_nn(left, right):
    return lax.dot_general(left, right, (((1,), (0,)), ((), ())), preferred_element_type=F32)


def dot_nt(left, right):
    return lax.dot_general(left, right, (((1,), (1,)), ((), ())), preferred_element_type=F32)


def rank_tables(me, dev, slot, cuts, tables):
    slices = dev.shape[1]
    per_block = slices // cuts
    source = lax.broadcasted_iota(jnp.int32, (cuts, slices), 0)
    low = lax.broadcasted_iota(jnp.int32, (slices, slices), 0)
    high = lax.broadcasted_iota(jnp.int32, (slices, slices), 1)
    same = low // per_block == high // per_block
    block = jnp.where(same, 1.0, 0.0).astype(BF16)
    before = jnp.where(same & (low < high), 1.0, 0.0).astype(BF16)
    hit0 = jnp.where(dev[0:1] == source, 1.0, 0.0)
    hit1 = jnp.where(dev[1:2] == source, 1.0, 0.0)
    rank0 = dot_nn(hit0.astype(BF16), before)
    rank1 = dot_nn(hit1.astype(BF16), before) + dot_nn(hit0.astype(BF16), block)
    rank0 = jnp.sum(hit0 * rank0, axis=0, keepdims=True)
    rank1 = jnp.sum(hit1 * rank1, axis=0, keepdims=True)
    arrival0 = dev[0:1] * CAP + rank0.astype(jnp.int32)
    arrival1 = dev[1:2] * CAP + rank1.astype(jnp.int32)
    tables[0:1, :] = arrival0
    tables[1:2, :] = arrival1
    wanted = lax.broadcasted_iota(jnp.int32, (8, slices), 0).astype(F32)
    mine0 = (dev[0:1] == me) & (rank0 == wanted)
    mine1 = (dev[1:2] == me) & (rank1 == wanted)
    slots = jnp.where(mine0, slot[0:1].astype(F32), 0.0) + jnp.where(mine1, slot[1:2].astype(F32), 0.0)
    place = lax.broadcasted_iota(jnp.int32, (slices, LANES), 0) // per_block
    column = lax.broadcasted_iota(jnp.int32, (slices, LANES), 1)
    chosen = dot_nn(slots.astype(BF16), jnp.where(place == column, 1.0, 0.0).astype(BF16))
    tables[8:16, 0:LANES] = chosen.astype(jnp.int32)


def section_kernel(
    cuts,
    tiles,
    theta_ref,
    dev_ref,
    slot_ref,
    weight_ref,
    coupling_ref,
    field_hbm,
    prop_hbm,
    cellx_hbm,
    celly_hbm,
    out_ref,
    field_v,
    prop_v,
    cellx_v,
    celly_v,
    tables_v,
    tables_s,
    phase_v,
    outgoing,
    arrived,
    row_code,
    col_code,
    full,
    round_send,
    source_send,
    hop,
    round_recv,
    source_recv,
    wide,
    tall,
    diff,
    back_send,
    back_recv,
    local_sem,
    theta_ss,
    theta_rs,
    round_ss,
    round_rs,
    source_ss,
    source_rs,
    hop_ss,
    hop_rs,
    back_ss,
    back_rs,
):
    c = lax.axis_index("cuts")
    t = lax.axis_index("tile")
    slots = theta_ref.shape[0]
    share = theta_ref.shape[1]
    pieces = share // LANES
    grid = prop_v.shape[1]
    rows = grid // tiles
    parts = 2 * rows

    barrier = pltpu.get_barrier_semaphore()

    def greet_cut(step, carry):
        pl.semaphore_signal(barrier, inc=1, device_id=(lax.rem(c + step, cuts), t), device_id_type=MESH)
        return carry

    def greet_tile(step, carry):
        pl.semaphore_signal(barrier, inc=1, device_id=(c, lax.rem(t + step, tiles)), device_id_type=MESH)
        return carry

    lax.fori_loop(1, cuts, greet_cut, 0)
    lax.fori_loop(1, tiles, greet_tile, 0)

    loads = [
        pltpu.make_async_copy(cellx_hbm, cellx_v, local_sem.at[0]),
        pltpu.make_async_copy(celly_hbm, celly_v, local_sem.at[1]),
        pltpu.make_async_copy(prop_hbm, prop_v, local_sem.at[2]),
    ] + [
        pltpu.make_async_copy(
            field_hbm.at[:, pl.ds(q * LANES, LANES)], field_v.at[q, pl.ds(0, 2 * slots * rows)], local_sem.at[3 + q]
        )
        for q in range(grid // LANES)
    ]
    for load in loads:
        load.start()

    rank_tables(c, dev_ref[...], slot_ref[...], cuts, tables_v)
    to_scalar = pltpu.make_async_copy(tables_v, tables_s, local_sem.at[6])
    to_scalar.start()

    turns = theta_ref[...] * (HARM / (2.0 * math.pi))
    turns = turns - jnp.floor(turns + 0.5)
    turns = jnp.minimum(jnp.floor(turns * 65536.0 + 0.5), 32767.0)
    for piece in range(pieces):
        phase_v[:, piece, :] = turns[:, piece * LANES : (piece + 1) * LANES]
    to_scalar.wait()

    def pick(block, carry):
        for rank in range(CAP):
            chosen = jnp.clip(tables_s[8 + rank, block], 0, slots - 1)
            outgoing[block * CAP + rank] = phase_v[chosen].astype(jnp.int32).astype(jnp.int16)
        return carry

    lax.fori_loop(0, cuts, pick, 0)
    pl.semaphore_wait(barrier, cuts + tiles - 2)

    def theta_copy(to, slot_of, sem_of):
        return pltpu.make_async_remote_copy(
            src_ref=outgoing.at[pl.ds(to * CAP, CAP)],
            dst_ref=arrived.at[pl.ds(slot_of * CAP, CAP)],
            send_sem=theta_ss.at[to],
            recv_sem=theta_rs.at[sem_of],
            device_id=(to, t),
            device_id_type=MESH,
        )

    def theta_start(step, carry):
        theta_copy(lax.rem(c + step, cuts), c, c).start()
        return carry

    lax.fori_loop(1, cuts, theta_start, 0)
    own_theta = pltpu.make_async_copy(
        outgoing.at[pl.ds(c * CAP, CAP)], arrived.at[pl.ds(c * CAP, CAP)], theta_rs.at[c]
    )
    own_theta.start()

    loads[0].wait()
    loads[1].wait()

    def codes(index, carry):
        cell_x = cellx_v[index]
        cell_y = celly_v[index]
        code = (cell_y // LANES) * rows + cell_x
        column = cell_y % LANES
        for k in range(2):
            row_code[2 * index + k] = jnp.broadcast_to(code[k : k + 1].astype(F32), (16, share)).astype(BF16)
            col_code[2 * index + k] = jnp.broadcast_to(column[k : k + 1].astype(F32), (16, share)).astype(BF16)
        return carry

    lax.fori_loop(0, slots, codes, 0)
    loads[2].wait()
    full[0:grid, 0:grid] = prop_v[0]
    full[0:grid, grid:] = -prop_v[1]
    full[grid:, 0:grid] = prop_v[1]
    full[grid:, grid:] = prop_v[0]
    for load in loads[3:]:
        load.wait()

    own_theta.wait()

    def theta_end(step, carry):
        other = lax.rem(c + step, cuts)
        theta_copy(other, other, other).wait_recv()
        return carry

    lax.fori_loop(1, cuts, theta_end, 0)

    width = 4 * LANES
    subs = lax.broadcasted_iota(jnp.int32, (16, width), 0)
    levels = [(subs + 16 * level).astype(F32).astype(BF16) for level in range(8)]
    one = jnp.ones((16, width), BF16)
    zero = jnp.zeros((16, width), BF16)
    c0r, c0i = coupling_ref[0, 0], coupling_ref[0, 1]
    c1r, c1i = coupling_ref[1, 0], coupling_ref[1, 1]

    def emit(slot):
        total = None
        for k in range(2):
            entry = c * slots + slot
            row = jnp.clip(tables_s[k, entry], 0, cuts * CAP - 1)
            weight = weight_ref[k, entry]
            phase = arrived[row].astype(jnp.int32).astype(F32) * (1.0 / 32768.0)
            cosine = sin_pi(0.5 - jnp.abs(phase))
            sine = sin_pi(jnp.maximum(jnp.minimum(phase, 1.0 - phase), -1.0 - phase))
            value_re = weight * cosine
            value_im = weight * sine
            index = 2 * slot + k
            for group in range(pieces // 4):
                lanes = slice(group * width, (group + 1) * width)
                column = col_code[index, :, lanes]
                code = row_code[index, :, lanes]
                spread_re = jnp.concatenate(
                    [jnp.broadcast_to(value_re[4 * group + i : 4 * group + i + 1], (16, LANES)) for i in range(4)], 1
                ).astype(BF16)
                spread_im = jnp.concatenate(
                    [jnp.broadcast_to(value_im[4 * group + i : 4 * group + i + 1], (16, LANES)) for i in range(4)], 1
                ).astype(BF16)
                hits = [code == level for level in levels[:5]]
                left = jnp.concatenate(
                    [jnp.where(hit, spread_re, zero) for hit in hits]
                    + [jnp.where(hit, spread_im, zero) for hit in hits],
                    0,
                )
                right = jnp.concatenate([jnp.where(column == level, one, zero) for level in levels], 0)
                product = dot_nt(left, right)
                total = product if total is None else total + product
        real_part = jnp.concatenate([total[i * rows : (i + 1) * rows] for i in range(3)], 1)
        imag_part = jnp.concatenate([total[80 + i * rows : 80 + (i + 1) * rows] for i in range(3)], 1)
        source = jnp.concatenate([real_part, imag_part], 0).astype(BF16)
        source_send[slot] = source
        source = source.astype(F32)
        real_part, imag_part = source[:rows], source[rows:]
        field_re = jnp.concatenate(
            [field_v[q, pl.ds(slot, rows, stride=2 * slots), :] for q in range(grid // LANES)], 1
        )
        field_im = jnp.concatenate(
            [field_v[q, pl.ds(slot + slots, rows, stride=2 * slots), :] for q in range(grid // LANES)], 1
        )
        sum_re = field_re + c0r * real_part - c0i * imag_part
        sum_im = field_im + c0r * imag_part + c0i * real_part
        round_send[slot] = jnp.concatenate([sum_re, sum_im], 0).astype(BF16)

    def hop_copy(which, src):
        return pltpu.make_async_remote_copy(
            src_ref=src,
            dst_ref=hop.at[which],
            send_sem=hop_ss.at[which],
            recv_sem=hop_rs.at[which],
            device_id=(lax.rem(c + 1, cuts), t),
            device_id_type=MESH,
        )

    def block_copy(src, dst, to, send, recv, sem_of):
        return pltpu.make_async_remote_copy(
            src_ref=src,
            dst_ref=dst,
            send_sem=send.at[to],
            recv_sem=recv.at[sem_of],
            device_id=(c, to),
            device_id_type=MESH,
        )

    def deliver(src, dst, to, send, recv):
        @pl.when(to == t)
        def _():
            pltpu.make_async_copy(src, dst.at[t], recv.at[t]).start()

        @pl.when(to != t)
        def _():
            block_copy(src, dst.at[t], to, send, recv, t).start()

    emit(slots - 1)
    hop_copy(1, round_send.at[slots - 1]).start()
    hop_copy(2, source_send.at[slots - 1]).start()
    emit(slots - 2)
    hop_copy(0, round_send.at[slots - 2]).start()
    deliver(source_send.at[slots - 2], source_recv, slots - 1, source_ss, source_rs)

    def forward():
        hop_copy(0, round_send.at[0]).wait_recv()
        deliver(hop.at[0], round_recv, 0, round_ss, round_rs)
        hop_copy(1, round_send.at[0]).wait_recv()
        deliver(hop.at[1], round_recv, 1, round_ss, round_rs)
        hop_copy(2, source_send.at[0]).wait_recv()
        deliver(hop.at[2], source_recv, 0, source_ss, source_rs)

    def one_slot(step, carry):
        slot = lax.rem(t + step, slots - 2)
        emit(slot)
        deliver(round_send.at[slot], round_recv, slot + 2, round_ss, round_rs)
        deliver(source_send.at[slot], source_recv, slot + 1, source_ss, source_rs)

        @pl.when(step == 5)
        def _():
            forward()

        return carry

    lax.fori_loop(0, slots - 2, one_slot, 0)

    def receive(src, dst, send, recv):
        pltpu.make_async_copy(src.at[0], dst.at[t], recv.at[t]).wait()

        def one(step, carry):
            other = lax.rem(t + step, tiles)
            block_copy(src.at[0], dst.at[other], other, send, recv, other).wait_recv()
            return carry

        lax.fori_loop(1, tiles, one, 0)

    receive(round_send, round_recv, round_ss, round_rs)

    def pair_of(ref, pair):
        first = ref[2 * pair].astype(F32)
        second = ref[2 * pair + 1].astype(F32)
        real_part = jnp.concatenate([first[:rows], second[:rows]], 0)
        imag_part = jnp.concatenate([first[rows:], second[rows:]], 0)
        return real_part, imag_part

    for pair in range(tiles // 2):
        real_part, imag_part = pair_of(round_recv, pair)
        wide[pair * parts : (pair + 1) * parts, 0:grid] = real_part.astype(BF16)
        wide[pair * parts : (pair + 1) * parts, grid:] = imag_part.astype(BF16)
    inter = dot_nt(wide[...], full[...])
    tall[0:grid, :] = inter[:, 0:grid].astype(BF16)
    tall[grid:, :] = inter[:, grid:].astype(BF16)
    diff[...] = dot_nn(full[...], tall[...])
    receive(source_send, source_recv, source_ss, source_rs)
    for pair in range(tiles // 2):
        real_part, imag_part = pair_of(source_recv, pair)
        top = slice(pair * parts, (pair + 1) * parts)
        low = slice(grid + pair * parts, grid + (pair + 1) * parts)
        tall[top, :] = (diff[top, :] + c1r * real_part - c1i * imag_part).astype(BF16)
        tall[low, :] = (diff[low, :] + c1r * imag_part + c1i * real_part).astype(BF16)

    def chunk_out(step, carry):
        chunk = lax.rem(t // 4 + step, tiles // 4)
        start = pl.multiple_of(chunk * 4 * rows, 4 * rows)
        inter_re = dot_nn(full[pl.ds(start, 4 * rows), :], tall[...])
        inter_im = dot_nn(full[pl.ds(start + grid, 4 * rows), :], tall[...])
        for i in range(4):
            to = 4 * chunk + i
            back_send[to] = jnp.concatenate(
                [inter_re[i * rows : (i + 1) * rows], inter_im[i * rows : (i + 1) * rows]], 0
            ).astype(BF16)
            deliver(back_send.at[to], back_recv, to, back_ss, back_rs)
        return carry

    lax.fori_loop(0, tiles // 4, chunk_out, 0)
    receive(back_send, back_recv, back_ss, back_rs)

    for slot in range(slots):
        block = back_recv[slot].astype(F32)
        for q in range(grid // LANES):
            lanes = slice(q * LANES, (q + 1) * LANES)
            field_v[q, pl.ds(slot, rows, stride=slots), :] = block[:rows, lanes]
            field_v[q, pl.ds(grid + slot, rows, stride=slots), :] = block[rows:, lanes]
    for q in range(grid // LANES):
        out_ref[:, q * LANES : (q + 1) * LANES] = field_v[q, 0:grid, :].astype(BF16)
        out_ref[:, grid + q * LANES : grid + (q + 1) * LANES] = field_v[q, grid : 2 * grid, :].astype(BF16)

    def sent_theta(step, carry):
        other = lax.rem(c + step, cuts)
        theta_copy(other, other, other).wait_send()
        return carry

    lax.fori_loop(1, cuts, sent_theta, 0)

    def sent(step, carry):
        other = lax.rem(t + step, tiles)
        block_copy(round_send.at[0], round_recv.at[0], other, round_ss, round_rs, other).wait_send()
        block_copy(source_send.at[0], source_recv.at[0], other, source_ss, source_rs, other).wait_send()
        block_copy(back_send.at[0], back_recv.at[0], other, back_ss, back_rs, other).wait_send()
        return carry

    lax.fori_loop(1, tiles, sent, 0)
    for which in range(3):
        hop_copy(which, round_send.at[0]).wait_send()


def final_kernel(wide_ref, prop_ref, out_ref):
    grid = prop_ref.shape[1]
    rows, _, slots, _ = out_ref.shape
    real_part = wide_ref[:, 0:grid]
    imag_part = wide_ref[:, grid:]
    out_re = dot_nt(real_part, prop_ref[0]) - dot_nt(imag_part, prop_ref[1])
    out_ref[:, 0] = out_re.reshape(rows, slots, grid)
    out_im = dot_nt(imag_part, prop_ref[0]) + dot_nt(real_part, prop_ref[1])
    out_ref[:, 1] = out_im.reshape(rows, slots, grid)


def on_device(cuts, tiles, field_in, propagator, theta, cell_x, cell_y, src_dev, src_slot, weights, coupling):
    grid = propagator.shape[1]
    rows = grid // tiles
    slots, share = theta.shape
    vmem = pl.BlockSpec(memory_space=pltpu.VMEM)
    smem = pl.BlockSpec(memory_space=pltpu.SMEM)
    anywhere = pl.BlockSpec(memory_space=pl.ANY)
    block = (2 * rows, grid)
    dma = pltpu.SemaphoreType.DMA
    wide = pl.pallas_call(
        functools.partial(section_kernel, cuts, tiles),
        out_shape=jax.ShapeDtypeStruct((grid, 2 * grid), BF16),
        in_specs=[vmem, vmem, vmem, smem, smem, anywhere, anywhere, anywhere, anywhere],
        out_specs=vmem,
        scratch_shapes=[
            pltpu.VMEM((grid // LANES, (rows + 1) * 2 * slots, LANES), F32),
            pltpu.VMEM((2, grid, grid), BF16),
            pltpu.VMEM((slots, 2, share), jnp.int32),
            pltpu.VMEM((slots, 2, share), jnp.int32),
            pltpu.VMEM((16, src_dev.shape[0]), jnp.int32),
            pltpu.SMEM((16, src_dev.shape[0]), jnp.int32),
            pltpu.VMEM((slots, share // LANES, LANES), F32),
            pltpu.VMEM((cuts * CAP, share // LANES, LANES), jnp.int16),
            pltpu.VMEM((cuts * CAP, share // LANES, LANES), jnp.int16),
            pltpu.VMEM((2 * slots, 16, share), BF16),
            pltpu.VMEM((2 * slots, 16, share), BF16),
            pltpu.VMEM((2 * grid, 2 * grid), BF16),
            pltpu.VMEM((slots,) + block, BF16),
            pltpu.VMEM((slots,) + block, BF16),
            pltpu.VMEM((3,) + block, BF16),
            pltpu.VMEM((tiles,) + block, BF16),
            pltpu.VMEM((tiles,) + block, BF16),
            pltpu.VMEM((grid, 2 * grid), BF16),
            pltpu.VMEM((2 * grid, grid), BF16),
            pltpu.VMEM((2 * grid, grid), F32),
            pltpu.VMEM((tiles,) + block, BF16),
            pltpu.VMEM((tiles,) + block, BF16),
            dma((7,)),
            dma((cuts,)),
            dma((cuts,)),
            dma((tiles,)),
            dma((tiles,)),
            dma((tiles,)),
            dma((tiles,)),
            dma((3,)),
            dma((3,)),
            dma((tiles,)),
            dma((tiles,)),
        ],
        compiler_params=pltpu.CompilerParams(
            collective_id=0, has_side_effects=True, vmem_limit_bytes=48 * 1024 * 1024
        ),
    )(
        theta,
        src_dev.T,
        src_slot.T,
        weights.T,
        coupling,
        field_in.reshape(rows * 2 * slots, grid),
        propagator,
        cell_x,
        cell_y,
    )
    return pl.pallas_call(
        final_kernel,
        out_shape=jax.ShapeDtypeStruct((rows, 2, slots, grid), F32),
        in_specs=[vmem, vmem],
        out_specs=vmem,
        compiler_params=pltpu.CompilerParams(vmem_limit_bytes=32 * 1024 * 1024),
    )(wide, propagator)


def solution(mesh):
    in_specs = (
        P("tile", None, "cuts", None),
        P(),
        P("cuts", "tile"),
        P("cuts", None, "tile"),
        P("cuts", None, "tile"),
        P(),
        P(),
        P(),
        P(),
    )
    out_specs = P("tile", None, "cuts", None)
    run = functools.partial(on_device, mesh.shape["cuts"], mesh.shape["tile"])
    return jax.shard_map(run, mesh=mesh, in_specs=in_specs, out_specs=out_specs, check_vma=False)
```

```python
import functools
import math

import jax
import jax.numpy as jnp
from jax import lax
from jax.experimental import pallas as pl
from jax.experimental.pallas import tpu as pltpu
from jax.sharding import PartitionSpec as P

HARM = 5
CAP = 4
LANES = 128
MESH = pl.DeviceIdType.MESH
SIN_PI = (
    3.141592502593994,
    -5.1677069664001465,
    2.5500311851501465,
    -0.5980440974235535,
    0.07721816748380661,
)
F32 = jnp.float32
BF16 = jnp.bfloat16


def sin_pi(fraction):
    square = fraction * fraction
    total = jnp.full_like(square, SIN_PI[4])
    for coefficient in SIN_PI[3::-1]:
        total = total * square + coefficient
    return total * fraction


def dot_nn(left, right):
    return lax.dot_general(left, right, (((1,), (0,)), ((), ())), preferred_element_type=F32)


def dot_nt(left, right):
    return lax.dot_general(left, right, (((1,), (1,)), ((), ())), preferred_element_type=F32)


def rank_tables(me, dev, slot, cuts, tables):
    slices = dev.shape[1]
    per_block = slices // cuts
    source = lax.broadcasted_iota(jnp.int32, (cuts, slices), 0)
    low = lax.broadcasted_iota(jnp.int32, (slices, slices), 0)
    high = lax.broadcasted_iota(jnp.int32, (slices, slices), 1)
    same = low // per_block == high // per_block
    block = jnp.where(same, 1.0, 0.0).astype(BF16)
    before = jnp.where(same & (low < high), 1.0, 0.0).astype(BF16)
    hit0 = jnp.where(dev[0:1] == source, 1.0, 0.0)
    hit1 = jnp.where(dev[1:2] == source, 1.0, 0.0)
    rank0 = dot_nn(hit0.astype(BF16), before)
    rank1 = dot_nn(hit1.astype(BF16), before) + dot_nn(hit0.astype(BF16), block)
    rank0 = jnp.sum(hit0 * rank0, axis=0, keepdims=True)
    rank1 = jnp.sum(hit1 * rank1, axis=0, keepdims=True)
    arrival0 = dev[0:1] * CAP + rank0.astype(jnp.int32)
    arrival1 = dev[1:2] * CAP + rank1.astype(jnp.int32)
    tables[0:1, :] = arrival0
    tables[1:2, :] = arrival1
    wanted = lax.broadcasted_iota(jnp.int32, (8, slices), 0).astype(F32)
    mine0 = (dev[0:1] == me) & (rank0 == wanted)
    mine1 = (dev[1:2] == me) & (rank1 == wanted)
    slots = jnp.where(mine0, slot[0:1].astype(F32), 0.0) + jnp.where(mine1, slot[1:2].astype(F32), 0.0)
    place = lax.broadcasted_iota(jnp.int32, (slices, LANES), 0) // per_block
    column = lax.broadcasted_iota(jnp.int32, (slices, LANES), 1)
    chosen = dot_nn(slots.astype(BF16), jnp.where(place == column, 1.0, 0.0).astype(BF16))
    tables[8:16, 0:LANES] = chosen.astype(jnp.int32)


def section_kernel(
    cuts,
    tiles,
    theta_hbm,
    dev_hbm,
    slot_hbm,
    weight_hbm,
    coupling_hbm,
    field_hbm,
    prop_hbm,
    cellx_hbm,
    celly_hbm,
    out_hbm,
    theta_ref,
    dev_ref,
    slot_ref,
    weight_ref,
    coupling_ref,
    field_v,
    prop_v,
    cellx_v,
    celly_v,
    tables_v,
    tables_s,
    phase_v,
    outgoing,
    arrived,
    row_code,
    col_code,
    full,
    field_send,
    source_send,
    field_hop,
    source_hop,
    field_recv,
    near_recv,
    far_recv,
    tall,
    diff,
    back_send,
    back_recv,
    local_sem,
    theta_ss,
    theta_rs,
    field_ss,
    field_rs,
    near_ss,
    near_rs,
    far_ss,
    far_rs,
    twin_ss,
    hop_ss,
    hop_rs,
    back_ss,
    back_rs,
):
    c = lax.axis_index("cuts")
    t = lax.axis_index("tile")
    slots = theta_ref.shape[0]
    share = theta_ref.shape[1]
    pieces = share // LANES
    grid = prop_v.shape[1]
    rows = grid // tiles
    parts = 2 * rows
    columns = grid // LANES
    groups = tiles // 4
    field_rows = 2 * slots * rows

    first = [
        pltpu.make_async_copy(dev_hbm, dev_ref, local_sem.at[0]),
        pltpu.make_async_copy(slot_hbm, slot_ref, local_sem.at[1]),
        pltpu.make_async_copy(theta_hbm, theta_ref, local_sem.at[2]),
        pltpu.make_async_copy(weight_hbm, weight_ref, local_sem.at[3]),
        pltpu.make_async_copy(coupling_hbm, coupling_ref, local_sem.at[4]),
        pltpu.make_async_copy(cellx_hbm, cellx_v, local_sem.at[5]),
        pltpu.make_async_copy(celly_hbm, celly_v, local_sem.at[6]),
        pltpu.make_async_copy(prop_hbm, prop_v, local_sem.at[7]),
    ]
    field_loads = [
        pltpu.make_async_copy(
            field_hbm.at[:, pl.ds(q * LANES, LANES)], field_v.at[q, pl.ds(0, field_rows)], local_sem.at[8 + q]
        )
        for q in range(columns)
    ]
    for load in first + field_loads:
        load.start()
    barrier = pltpu.get_barrier_semaphore()

    def greet_cut(step, carry):
        pl.semaphore_signal(barrier, inc=1, device_id=(lax.rem(c + step, cuts), t), device_id_type=MESH)
        return carry

    def greet_tile(step, carry):
        pl.semaphore_signal(barrier, inc=1, device_id=(c, lax.rem(t + step, tiles)), device_id_type=MESH)
        return carry

    lax.fori_loop(1, cuts, greet_cut, 0)
    lax.fori_loop(1, tiles, greet_tile, 0)

    first[0].wait()
    first[1].wait()
    rank_tables(c, dev_ref[...], slot_ref[...], cuts, tables_v)
    to_scalar = pltpu.make_async_copy(tables_v, tables_s, local_sem.at[11])
    to_scalar.start()

    first[2].wait()
    turns = theta_ref[...] * (HARM / (2.0 * math.pi))
    turns = turns - jnp.floor(turns + 0.5)
    turns = jnp.minimum(jnp.floor(turns * 65536.0 + 0.5), 32767.0)
    for piece in range(pieces):
        phase_v[:, piece, :] = turns[:, piece * LANES : (piece + 1) * LANES]
    def hop_copy(which, src, dst):
        return pltpu.make_async_remote_copy(
            src_ref=src,
            dst_ref=dst,
            send_sem=hop_ss.at[which],
            recv_sem=hop_rs.at[which],
            device_id=(lax.rem(c + 1, cuts), t),
            device_id_type=MESH,
        )

    def block_copy(src, dst, to, send, recv):
        return pltpu.make_async_remote_copy(
            src_ref=src, dst_ref=dst, send_sem=send, recv_sem=recv, device_id=(c, to), device_id_type=MESH
        )

    def deliver(src, dst, to, send, recv):
        @pl.when(to == t)
        def _():
            pltpu.make_async_copy(src, dst.at[t], recv.at[t]).start()

        @pl.when(to != t)
        def _():
            block_copy(src, dst.at[t], to, send.at[to], recv.at[t]).start()

    def arrive(dst, other, recv):
        block_copy(back_send.at[0], dst.at[other], other, back_ss.at[0], recv.at[other]).wait_recv()

    def stage_field(slot):
        pieces_re = [field_v[q, pl.ds(slot, rows, stride=2 * slots), :] for q in range(columns)]
        pieces_im = [field_v[q, pl.ds(slot + slots, rows, stride=2 * slots), :] for q in range(columns)]
        field_send[slot] = jnp.concatenate(
            [jnp.concatenate(pieces_re, 1), jnp.concatenate(pieces_im, 1)], 0
        ).astype(BF16)

    for load in field_loads:
        load.wait()
    stage_field(slots - 2)
    stage_field(slots - 1)
    pl.semaphore_wait(barrier, cuts + tiles - 2)
    for which in range(2):
        hop_copy(which, field_send.at[slots - 2 + which], field_hop.at[which]).start()
    to_scalar.wait()

    def pick(block, carry):
        for rank in range(CAP):
            chosen = jnp.clip(tables_s[8 + rank, block], 0, slots - 1)
            outgoing[block * CAP + rank] = phase_v[chosen].astype(jnp.int32).astype(jnp.int16)
        return carry

    lax.fori_loop(0, cuts, pick, 0)

    def theta_copy(to, slot_of, sem_of):
        return pltpu.make_async_remote_copy(
            src_ref=outgoing.at[pl.ds(to * CAP, CAP)],
            dst_ref=arrived.at[pl.ds(slot_of * CAP, CAP)],
            send_sem=theta_ss.at[to],
            recv_sem=theta_rs.at[sem_of],
            device_id=(to, t),
            device_id_type=MESH,
        )

    def theta_start(step, carry):
        theta_copy(lax.rem(c + step, cuts), c, c).start()
        return carry

    lax.fori_loop(1, cuts, theta_start, 0)
    own_theta = pltpu.make_async_copy(
        outgoing.at[pl.ds(c * CAP, CAP)], arrived.at[pl.ds(c * CAP, CAP)], theta_rs.at[c]
    )
    own_theta.start()

    def one_field(step, carry):
        slot = lax.rem(t + step, slots - 2)
        stage_field(slot)
        deliver(field_send.at[slot], field_recv, slot + 2, field_ss, field_rs)
        return carry

    lax.fori_loop(0, slots - 2, one_field, 0)
    for which in range(2):
        hop_copy(which, field_send.at[0], field_hop.at[which]).wait_recv()
        deliver(field_hop.at[which], field_recv, which, field_ss, field_rs)

    for load in first[3:]:
        load.wait()

    def codes(index, carry):
        cell_x = cellx_v[index]
        cell_y = celly_v[index]
        code = (cell_y // LANES) * rows + cell_x
        column = cell_y % LANES
        for k in range(2):
            row_code[2 * index + k] = jnp.broadcast_to(code[k : k + 1].astype(F32), (16, share)).astype(BF16)
            col_code[2 * index + k] = jnp.broadcast_to(column[k : k + 1].astype(F32), (16, share)).astype(BF16)
        return carry

    lax.fori_loop(0, slots, codes, 0)
    full[0:grid, 0:grid] = prop_v[0]
    full[0:grid, grid:] = -prop_v[1]
    full[grid:, 0:grid] = prop_v[1]
    full[grid:, grid:] = prop_v[0]

    own_theta.wait()

    def theta_end(step, carry):
        other = lax.rem(c + step, cuts)
        theta_copy(other, other, other).wait_recv()
        return carry

    lax.fori_loop(1, cuts, theta_end, 0)

    width = 4 * LANES
    subs = lax.broadcasted_iota(jnp.int32, (16, width), 0)
    levels = [(subs + 16 * level).astype(F32).astype(BF16) for level in range(8)]
    one = jnp.ones((16, width), BF16)
    zero = jnp.zeros((16, width), BF16)
    c0r, c0i = coupling_ref[0, 0], coupling_ref[0, 1]
    c1r, c1i = coupling_ref[1, 0], coupling_ref[1, 1]

    def deposit(slot):
        total = None
        for k in range(2):
            entry = c * slots + slot
            row = jnp.clip(tables_s[k, entry], 0, cuts * CAP - 1)
            weight = weight_ref[k, entry]
            phase = arrived[row].astype(jnp.int32).astype(F32) * (1.0 / 32768.0)
            cosine = sin_pi(0.5 - jnp.abs(phase))
            sine = sin_pi(jnp.maximum(jnp.minimum(phase, 1.0 - phase), -1.0 - phase))
            value_re = weight * cosine
            value_im = weight * sine
            index = 2 * slot + k
            for group in range(pieces // 4):
                lanes = slice(group * width, (group + 1) * width)
                column = col_code[index, :, lanes]
                code = row_code[index, :, lanes]
                spread_re = jnp.concatenate(
                    [jnp.broadcast_to(value_re[4 * group + i : 4 * group + i + 1], (16, LANES)) for i in range(4)], 1
                ).astype(BF16)
                spread_im = jnp.concatenate(
                    [jnp.broadcast_to(value_im[4 * group + i : 4 * group + i + 1], (16, LANES)) for i in range(4)], 1
                ).astype(BF16)
                hits = [code == level for level in levels[:5]]
                left = jnp.concatenate(
                    [jnp.where(hit, spread_re, zero) for hit in hits]
                    + [jnp.where(hit, spread_im, zero) for hit in hits],
                    0,
                )
                right = jnp.concatenate([jnp.where(column == level, one, zero) for level in levels], 0)
                product = dot_nt(left, right)
                total = product if total is None else total + product
        real_part = jnp.concatenate([total[i * rows : (i + 1) * rows] for i in range(3)], 1)
        imag_part = jnp.concatenate([total[80 + i * rows : 80 + (i + 1) * rows] for i in range(3)], 1)
        source_send[slot] = jnp.concatenate([real_part, imag_part], 0).astype(BF16)

    deposit(slots - 1)
    hop_copy(3, source_send.at[slots - 1], source_hop.at[1]).start()
    deposit(slots - 2)
    hop_copy(2, source_send.at[slots - 2], source_hop.at[0]).start()
    deliver(source_send.at[slots - 2], near_recv, slots - 1, near_ss, near_rs)

    def one_slot(step, carry):
        slot = lax.rem(t + step, slots - 2)
        deposit(slot)
        deliver(source_send.at[slot], near_recv, slot + 1, near_ss, near_rs)

        @pl.when(lax.rem(slot, 2) == 0)
        def _():
            deliver(source_send.at[slot], far_recv, slot + 2, far_ss, far_rs)

        @pl.when(step == 4)
        def _():
            hop_copy(3, source_send.at[0], source_hop.at[1]).wait_recv()
            deliver(source_hop.at[1], near_recv, 0, near_ss, near_rs)
            hop_copy(2, source_send.at[0], source_hop.at[0]).wait_recv()
            deliver(source_hop.at[0], far_recv, 0, far_ss, far_rs)

        return carry

    lax.fori_loop(0, slots - 2, one_slot, 0)

    def field_in(other, carry):
        arrive(field_recv, other, field_rs)
        return carry

    lax.fori_loop(0, tiles, field_in, 0)
    even = lax.rem(t, 2) == 0
    twin = t + 1 - 2 * lax.rem(t, 2)

    def pair_of(ref, pair):
        first = ref[2 * pair].astype(F32)
        second = ref[2 * pair + 1].astype(F32)
        real_part = jnp.concatenate([first[:rows], second[:rows]], 0)
        imag_part = jnp.concatenate([first[rows:], second[rows:]], 0)
        return real_part, imag_part

    def first_period(step, carry):
        group = lax.rem((t + tiles - 1) // 4 + groups - step, groups)
        for i in range(3, -1, -1):
            other = 4 * group + i
            arrive(near_recv, other, near_rs)

            @pl.when(even)
            def _():
                block_copy(
                    near_recv.at[other], far_recv.at[other], twin, twin_ss.at[other], far_rs.at[other]
                ).start()

        for i in range(3, -1, -1):
            arrive(far_recv, 4 * group + i, far_rs)
        blocks = []
        for i in range(2):
            field_re, field_im = pair_of(field_recv, 2 * group + i)
            source_re, source_im = pair_of(far_recv, 2 * group + i)
            sum_re = field_re + c0r * source_re - c0i * source_im
            sum_im = field_im + c0r * source_im + c0i * source_re
            blocks.append(jnp.concatenate([sum_re.astype(BF16), sum_im.astype(BF16)], 1))
        inter = dot_nt(jnp.concatenate(blocks, 0), full[...])
        start = pl.multiple_of(group * 4 * rows, 4 * rows)
        tall[pl.ds(start, 4 * rows), :] = inter[:, 0:grid].astype(BF16)
        tall[pl.ds(grid + start, 4 * rows), :] = inter[:, grid:].astype(BF16)
        return carry

    lax.fori_loop(0, groups, first_period, 0)
    diff[...] = dot_nn(full[...], tall[...])
    for pair in range(tiles // 2):
        real_part, imag_part = pair_of(near_recv, pair)
        top = slice(pair * parts, (pair + 1) * parts)
        low = slice(grid + pair * parts, grid + (pair + 1) * parts)
        tall[top, :] = (diff[top, :] + c1r * real_part - c1i * imag_part).astype(BF16)
        tall[low, :] = (diff[low, :] + c1r * imag_part + c1i * real_part).astype(BF16)

    def chunk_out(step, carry):
        chunk = lax.rem(t // 4 + step, groups)
        start = pl.multiple_of(chunk * 4 * rows, 4 * rows)
        inter_re = dot_nn(full[pl.ds(start, 4 * rows), :], tall[...])
        inter_im = dot_nn(full[pl.ds(start + grid, 4 * rows), :], tall[...])
        for i in range(4):
            to = 4 * chunk + i
            back_send[to] = jnp.concatenate(
                [inter_re[i * rows : (i + 1) * rows], inter_im[i * rows : (i + 1) * rows]], 0
            ).astype(BF16)
            deliver(back_send.at[to], back_recv, to, back_ss, back_rs)
        return carry

    lax.fori_loop(0, groups, chunk_out, 0)

    def last_period(step, carry):
        group = lax.rem(t // 4 + groups - step, groups)
        blocks = []
        for i in range(4):
            arrive(back_recv, 4 * group + i, back_rs)
        for i in range(2):
            real_part, imag_part = pair_of(back_recv, 2 * group + i)
            blocks.append(jnp.concatenate([real_part.astype(BF16), imag_part.astype(BF16)], 1))
        result = dot_nt(jnp.concatenate(blocks, 0), full[...])
        for i in range(4):
            slot = 4 * group + i
            for q in range(columns):
                for part in range(2):
                    at = part * grid + q * LANES
                    field_v[q, pl.ds(part * slots + slot, rows, stride=2 * slots), :] = result[
                        i * rows : (i + 1) * rows, at : at + LANES
                    ]
        return carry

    lax.fori_loop(0, groups, last_period, 0)
    stores = [
        pltpu.make_async_copy(
            field_v.at[q, pl.ds(0, field_rows)], out_hbm.at[:, pl.ds(q * LANES, LANES)], local_sem.at[8 + q]
        )
        for q in range(columns)
    ]
    for store in stores:
        store.start()

    def sent_theta(step, carry):
        other = lax.rem(c + step, cuts)
        theta_copy(other, other, other).wait_send()
        return carry

    lax.fori_loop(1, cuts, sent_theta, 0)

    def leave(to, send):
        block_copy(back_send.at[0], back_recv.at[0], to, send.at[to], back_rs.at[0]).wait_send()

    def sent(step, carry):
        other = lax.rem(t + step, tiles)
        leave(other, field_ss)
        leave(other, near_ss)
        leave(other, back_ss)

        @pl.when(lax.rem(other, 2) == 0)
        def _():
            leave(other, far_ss)

        return carry

    lax.fori_loop(1, tiles, sent, 0)

    @pl.when(even)
    def _():
        def sent_twin(other, carry):
            leave(other, twin_ss)
            return carry

        lax.fori_loop(0, tiles, sent_twin, 0)

    for which in range(2):
        hop_copy(which, field_send.at[0], field_hop.at[which]).wait_send()
        hop_copy(2 + which, source_send.at[0], source_hop.at[which]).wait_send()
    for store in stores:
        store.wait()


def on_device(cuts, tiles, field_in, propagator, theta, cell_x, cell_y, src_dev, src_slot, weights, coupling):
    grid = propagator.shape[1]
    rows = grid // tiles
    slots, share = theta.shape
    slices = src_dev.shape[0]
    hbm = pl.BlockSpec(memory_space=pltpu.HBM)
    block = (2 * rows, grid)
    blocks = pltpu.VMEM((tiles,) + block, BF16)
    dma = pltpu.SemaphoreType.DMA
    result = pl.pallas_call(
        functools.partial(section_kernel, cuts, tiles),
        out_shape=jax.ShapeDtypeStruct((rows * 2 * slots, grid), F32),
        in_specs=[hbm] * 9,
        out_specs=hbm,
        scratch_shapes=[
            pltpu.VMEM((slots, share), F32),
            pltpu.VMEM((2, slices), jnp.int32),
            pltpu.VMEM((2, slices), jnp.int32),
            pltpu.SMEM((2, slices), F32),
            pltpu.SMEM((2, 2), F32),
            pltpu.VMEM((grid // LANES, (rows + 1) * 2 * slots, LANES), F32),
            pltpu.VMEM((2, grid, grid), BF16),
            pltpu.VMEM((slots, 2, share), jnp.int32),
            pltpu.VMEM((slots, 2, share), jnp.int32),
            pltpu.VMEM((16, slices), jnp.int32),
            pltpu.SMEM((16, slices), jnp.int32),
            pltpu.VMEM((slots, share // LANES, LANES), F32),
            pltpu.VMEM((cuts * CAP, share // LANES, LANES), jnp.int16),
            pltpu.VMEM((cuts * CAP, share // LANES, LANES), jnp.int16),
            pltpu.VMEM((2 * slots, 16, share), BF16),
            pltpu.VMEM((2 * slots, 16, share), BF16),
            pltpu.VMEM((2 * grid, 2 * grid), BF16),
            blocks,
            blocks,
            pltpu.VMEM((2,) + block, BF16),
            pltpu.VMEM((2,) + block, BF16),
            blocks,
            blocks,
            blocks,
            pltpu.VMEM((2 * grid, grid), BF16),
            pltpu.VMEM((2 * grid, grid), F32),
            blocks,
            blocks,
            dma((12,)),
            dma((cuts,)),
            dma((cuts,)),
            dma((tiles,)),
            dma((tiles,)),
            dma((tiles,)),
            dma((tiles,)),
            dma((tiles,)),
            dma((tiles,)),
            dma((tiles,)),
            dma((4,)),
            dma((4,)),
            dma((tiles,)),
            dma((tiles,)),
        ],
        compiler_params=pltpu.CompilerParams(
            collective_id=0, has_side_effects=True, vmem_limit_bytes=64 * 1024 * 1024
        ),
    )(
        theta,
        src_dev.T,
        src_slot.T,
        weights.T,
        coupling,
        field_in.reshape(rows * 2 * slots, grid),
        propagator,
        cell_x,
        cell_y,
    )
    return result.reshape(rows, 2, slots, grid)


def solution(mesh):
    in_specs = (
        P("tile", None, "cuts", None),
        P(),
        P("cuts", "tile"),
        P("cuts", None, "tile"),
        P("cuts", None, "tile"),
        P(),
        P(),
        P(),
        P(),
    )
    out_specs = P("tile", None, "cuts", None)
    run = functools.partial(on_device, mesh.shape["cuts"], mesh.shape["tile"])
    return jax.shard_map(run, mesh=mesh, in_specs=in_specs, out_specs=out_specs, check_vma=False)
```

```python
import functools
import math

import jax
import jax.numpy as jnp
from jax import lax
from jax.experimental import pallas as pl
from jax.experimental.pallas import tpu as pltpu
from jax.sharding import PartitionSpec as P

HARM = 5
CAP = 4
LANES = 128
MESH = pl.DeviceIdType.MESH
SIN_PI = (
    3.141592502593994,
    -5.1677069664001465,
    2.5500311851501465,
    -0.5980440974235535,
    0.07721816748380661,
)
F32 = jnp.float32
BF16 = jnp.bfloat16


def sin_pi(fraction):
    square = fraction * fraction
    total = jnp.full_like(square, SIN_PI[4])
    for coefficient in SIN_PI[3::-1]:
        total = total * square + coefficient
    return total * fraction


def turn(step, count):
    return count // 2 + (1 - 2 * lax.rem(step, 2)) * ((step + 1) // 2)


def dot_nn(left, right):
    return lax.dot_general(left, right, (((1,), (0,)), ((), ())), preferred_element_type=F32)


def dot_nt(left, right):
    return lax.dot_general(left, right, (((1,), (1,)), ((), ())), preferred_element_type=F32)


def rank_tables(me, dev, slot, cuts, tables):
    slices = dev.shape[1]
    per_block = slices // cuts
    source = lax.broadcasted_iota(jnp.int32, (cuts, slices), 0)
    low = lax.broadcasted_iota(jnp.int32, (slices, slices), 0)
    high = lax.broadcasted_iota(jnp.int32, (slices, slices), 1)
    same = low // per_block == high // per_block
    block = jnp.where(same, 1.0, 0.0).astype(BF16)
    before = jnp.where(same & (low < high), 1.0, 0.0).astype(BF16)
    hit0 = jnp.where(dev[0:1] == source, 1.0, 0.0)
    hit1 = jnp.where(dev[1:2] == source, 1.0, 0.0)
    rank0 = dot_nn(hit0.astype(BF16), before)
    rank1 = dot_nn(hit1.astype(BF16), before) + dot_nn(hit0.astype(BF16), block)
    rank0 = jnp.sum(hit0 * rank0, axis=0, keepdims=True)
    rank1 = jnp.sum(hit1 * rank1, axis=0, keepdims=True)
    arrival0 = dev[0:1] * CAP + rank0.astype(jnp.int32)
    arrival1 = dev[1:2] * CAP + rank1.astype(jnp.int32)
    tables[0:1, :] = arrival0
    tables[1:2, :] = arrival1
    wanted = lax.broadcasted_iota(jnp.int32, (8, slices), 0).astype(F32)
    mine0 = (dev[0:1] == me) & (rank0 == wanted)
    mine1 = (dev[1:2] == me) & (rank1 == wanted)
    slots = jnp.where(mine0, slot[0:1].astype(F32), 0.0) + jnp.where(mine1, slot[1:2].astype(F32), 0.0)
    place = lax.broadcasted_iota(jnp.int32, (slices, LANES), 0) // per_block
    column = lax.broadcasted_iota(jnp.int32, (slices, LANES), 1)
    chosen = dot_nn(slots.astype(BF16), jnp.where(place == column, 1.0, 0.0).astype(BF16))
    tables[8:16, 0:LANES] = chosen.astype(jnp.int32)


def section_kernel(
    cuts,
    tiles,
    theta_hbm,
    dev_hbm,
    slot_hbm,
    weight_hbm,
    coupling_hbm,
    field_hbm,
    prop_hbm,
    cellx_hbm,
    celly_hbm,
    out_hbm,
    theta_ref,
    dev_ref,
    slot_ref,
    weight_ref,
    coupling_ref,
    field_v,
    prop_v,
    cellx_v,
    celly_v,
    tables_v,
    tables_s,
    phase_v,
    outgoing,
    arrived,
    row_code,
    col_code,
    full,
    field_send,
    source_send,
    field_hop,
    source_hop,
    field_recv,
    near_recv,
    far_recv,
    tall,
    diff,
    back_send,
    back_recv,
    local_sem,
    theta_ss,
    theta_rs,
    field_ss,
    field_rs,
    near_ss,
    near_rs,
    far_ss,
    far_rs,
    twin_ss,
    hop_ss,
    hop_rs,
    back_ss,
    back_rs,
):
    c = lax.axis_index("cuts")
    t = lax.axis_index("tile")
    slots = theta_ref.shape[0]
    share = theta_ref.shape[1]
    pieces = share // LANES
    grid = prop_v.shape[1]
    rows = grid // tiles
    parts = 2 * rows
    columns = grid // LANES
    groups = tiles // 4
    field_rows = 2 * slots * rows

    first = [
        pltpu.make_async_copy(dev_hbm, dev_ref, local_sem.at[0]),
        pltpu.make_async_copy(slot_hbm, slot_ref, local_sem.at[1]),
        pltpu.make_async_copy(theta_hbm, theta_ref, local_sem.at[2]),
        pltpu.make_async_copy(weight_hbm, weight_ref, local_sem.at[3]),
        pltpu.make_async_copy(coupling_hbm, coupling_ref, local_sem.at[4]),
        pltpu.make_async_copy(cellx_hbm, cellx_v, local_sem.at[5]),
        pltpu.make_async_copy(celly_hbm, celly_v, local_sem.at[6]),
        pltpu.make_async_copy(prop_hbm, prop_v, local_sem.at[7]),
    ]
    field_loads = [
        pltpu.make_async_copy(
            field_hbm.at[:, pl.ds(q * LANES, LANES)], field_v.at[q, pl.ds(0, field_rows)], local_sem.at[8 + q]
        )
        for q in range(columns)
    ]
    for load in first + field_loads:
        load.start()
    barrier = pltpu.get_barrier_semaphore()

    def greet_cut(step, carry):
        pl.semaphore_signal(barrier, inc=1, device_id=(lax.rem(c + step, cuts), t), device_id_type=MESH)
        return carry

    def greet_tile(step, carry):
        pl.semaphore_signal(barrier, inc=1, device_id=(c, lax.rem(t + step, tiles)), device_id_type=MESH)
        return carry

    lax.fori_loop(1, cuts, greet_cut, 0)
    lax.fori_loop(1, tiles, greet_tile, 0)
    pl.semaphore_signal(
        barrier, inc=1, device_id=(lax.rem(c + cuts - 1, cuts), tiles - 1), device_id_type=MESH
    )

    first[0].wait()
    first[1].wait()
    rank_tables(c, dev_ref[...], slot_ref[...], cuts, tables_v)
    to_scalar = pltpu.make_async_copy(tables_v, tables_s, local_sem.at[11])
    to_scalar.start()

    first[2].wait()
    turns = theta_ref[...] * (HARM / (2.0 * math.pi))
    turns = turns - jnp.floor(turns + 0.5)
    turns = jnp.minimum(jnp.floor(turns * 65536.0 + 0.5), 32767.0)
    for piece in range(pieces):
        phase_v[:, piece, :] = turns[:, piece * LANES : (piece + 1) * LANES]
    def hop_copy(which, src, dst):
        return pltpu.make_async_remote_copy(
            src_ref=src,
            dst_ref=dst,
            send_sem=hop_ss.at[which],
            recv_sem=hop_rs.at[which],
            device_id=(lax.rem(c + 1, cuts), t),
            device_id_type=MESH,
        )

    def block_copy(src, dst, to, send, recv):
        return pltpu.make_async_remote_copy(
            src_ref=src, dst_ref=dst, send_sem=send, recv_sem=recv, device_id=(c, to), device_id_type=MESH
        )

    def deliver(src, dst, to, send, recv, place=t):
        @pl.when(to == t)
        def _():
            pltpu.make_async_copy(src, dst.at[place], recv.at[place]).start()

        @pl.when(to != t)
        def _():
            block_copy(src, dst.at[place], to, send.at[to], recv.at[place]).start()

    def arrive(dst, other, recv):
        block_copy(back_send.at[0], dst.at[other], other, back_ss.at[0], recv.at[other]).wait_recv()

    def stage_field(slot):
        pieces_re = [field_v[q, pl.ds(slot, rows, stride=2 * slots), :] for q in range(columns)]
        pieces_im = [field_v[q, pl.ds(slot + slots, rows, stride=2 * slots), :] for q in range(columns)]
        field_send[slot] = jnp.concatenate(
            [jnp.concatenate(pieces_re, 1), jnp.concatenate(pieces_im, 1)], 0
        ).astype(BF16)

    for load in field_loads:
        load.wait()
    stage_field(slots - 1)
    pl.semaphore_wait(barrier, cuts + tiles - 2 + tiles * (t // (tiles - 1)))
    hop_copy(0, field_send.at[slots - 1], field_hop.at[0]).start()
    to_scalar.wait()

    def pick(block, carry):
        for rank in range(CAP):
            chosen = jnp.clip(tables_s[8 + rank, block], 0, slots - 1)
            outgoing[block * CAP + rank] = phase_v[chosen].astype(jnp.int32).astype(jnp.int16)
        return carry

    lax.fori_loop(0, cuts, pick, 0)

    def theta_copy(to, slot_of, sem_of):
        return pltpu.make_async_remote_copy(
            src_ref=outgoing.at[pl.ds(to * CAP, CAP)],
            dst_ref=arrived.at[pl.ds(slot_of * CAP, CAP)],
            send_sem=theta_ss.at[to],
            recv_sem=theta_rs.at[sem_of],
            device_id=(to, t),
            device_id_type=MESH,
        )

    def theta_start(step, carry):
        theta_copy(lax.rem(c + step, cuts), c, c).start()
        return carry

    lax.fori_loop(1, cuts, theta_start, 0)
    own_theta = pltpu.make_async_copy(
        outgoing.at[pl.ds(c * CAP, CAP)], arrived.at[pl.ds(c * CAP, CAP)], theta_rs.at[c]
    )
    own_theta.start()

    def one_field(step, carry):
        slot = lax.rem(t + turn(step, slots), slots)

        @pl.when(slot < slots - 1)
        def _():
            stage_field(slot)
            deliver(field_send.at[slot], field_recv, slot + 1, field_ss, field_rs)

        return carry

    lax.fori_loop(0, slots, one_field, 0)
    hop_copy(0, field_send.at[0], field_hop.at[0]).wait_recv()
    deliver(field_hop.at[0], field_recv, 0, field_ss, field_rs)

    for load in first[3:]:
        load.wait()

    def codes(index, carry):
        cell_x = cellx_v[index]
        cell_y = celly_v[index]
        code = (cell_y // LANES) * rows + cell_x
        column = cell_y % LANES
        for k in range(2):
            row_code[2 * index + k] = jnp.broadcast_to(code[k : k + 1].astype(F32), (16, share)).astype(BF16)
            col_code[2 * index + k] = jnp.broadcast_to(column[k : k + 1].astype(F32), (16, share)).astype(BF16)
        return carry

    lax.fori_loop(0, slots, codes, 0)
    full[0:grid, 0:grid] = prop_v[0]
    full[0:grid, grid:] = -prop_v[1]
    full[grid:, 0:grid] = prop_v[1]
    full[grid:, grid:] = prop_v[0]

    own_theta.wait()

    def theta_end(step, carry):
        other = lax.rem(c + step, cuts)
        theta_copy(other, other, other).wait_recv()
        return carry

    lax.fori_loop(1, cuts, theta_end, 0)

    width = 4 * LANES
    subs = lax.broadcasted_iota(jnp.int32, (16, width), 0)
    levels = [(subs + 16 * level).astype(F32).astype(BF16) for level in range(8)]
    one = jnp.ones((16, width), BF16)
    zero = jnp.zeros((16, width), BF16)
    c0r, c0i = coupling_ref[0, 0], coupling_ref[0, 1]
    c1r, c1i = coupling_ref[1, 0], coupling_ref[1, 1]

    def deposit(slot):
        total = None
        for k in range(2):
            entry = c * slots + slot
            row = jnp.clip(tables_s[k, entry], 0, cuts * CAP - 1)
            weight = weight_ref[k, entry]
            phase = arrived[row].astype(jnp.int32).astype(F32) * (1.0 / 32768.0)
            cosine = sin_pi(0.5 - jnp.abs(phase))
            sine = sin_pi(jnp.maximum(jnp.minimum(phase, 1.0 - phase), -1.0 - phase))
            value_re = weight * cosine
            value_im = weight * sine
            index = 2 * slot + k
            for group in range(pieces // 4):
                lanes = slice(group * width, (group + 1) * width)
                column = col_code[index, :, lanes]
                code = row_code[index, :, lanes]
                spread_re = jnp.concatenate(
                    [jnp.broadcast_to(value_re[4 * group + i : 4 * group + i + 1], (16, LANES)) for i in range(4)], 1
                ).astype(BF16)
                spread_im = jnp.concatenate(
                    [jnp.broadcast_to(value_im[4 * group + i : 4 * group + i + 1], (16, LANES)) for i in range(4)], 1
                ).astype(BF16)
                hits = [code == level for level in levels[:5]]
                left = jnp.concatenate(
                    [jnp.where(hit, spread_re, zero) for hit in hits]
                    + [jnp.where(hit, spread_im, zero) for hit in hits],
                    0,
                )
                right = jnp.concatenate([jnp.where(column == level, one, zero) for level in levels], 0)
                product = dot_nt(left, right)
                total = product if total is None else total + product
        real_part = jnp.concatenate([total[i * rows : (i + 1) * rows] for i in range(3)], 1)
        imag_part = jnp.concatenate([total[80 + i * rows : 80 + (i + 1) * rows] for i in range(3)], 1)
        source_send[slot] = jnp.concatenate([real_part, imag_part], 0).astype(BF16)

    deposit(slots - 1)
    hop_copy(1, source_send.at[slots - 1], source_hop.at[0]).start()
    deliver(source_send.at[slots - 1], near_recv, slots - 1, near_ss, near_rs)

    def one_slot(step, carry):
        slot = lax.rem(t + turn(step, slots), slots)

        @pl.when(slot < slots - 1)
        def _():
            deposit(slot)
            deliver(source_send.at[slot], far_recv, slot + 1, far_ss, far_rs)

        @pl.when((lax.rem(slot, 2) == 1) & (slot < slots - 1))
        def _():
            deliver(source_send.at[slot], near_recv, slot, near_ss, near_rs)

        @pl.when(step == 4)
        def _():
            hop_copy(1, source_send.at[0], source_hop.at[0]).wait_recv()
            deliver(source_hop.at[0], far_recv, 0, far_ss, far_rs)

        return carry

    lax.fori_loop(0, slots, one_slot, 0)

    def field_in(other, carry):
        arrive(field_recv, other, field_rs)
        return carry

    lax.fori_loop(0, tiles, field_in, 0)
    odd = lax.rem(t, 2) == 1

    def pair_of(ref, pair):
        first = ref[2 * pair].astype(F32)
        second = ref[2 * pair + 1].astype(F32)
        real_part = jnp.concatenate([first[:rows], second[:rows]], 0)
        imag_part = jnp.concatenate([first[rows:], second[rows:]], 0)
        return real_part, imag_part

    def first_period(step, carry):
        group = lax.rem(t // 4 + turn(step, groups), groups)
        for i in range(4):
            other = 4 * group + i
            arrive(far_recv, other, far_rs)

            @pl.when(odd)
            def _():
                block_copy(
                    far_recv.at[other], near_recv.at[other], t - 1, twin_ss.at[other], near_rs.at[other]
                ).start()

        blocks = []
        for i in range(2):
            field_re, field_im = pair_of(field_recv, 2 * group + i)
            source_re, source_im = pair_of(far_recv, 2 * group + i)
            sum_re = field_re + c0r * source_re - c0i * source_im
            sum_im = field_im + c0r * source_im + c0i * source_re
            blocks.append(jnp.concatenate([sum_re.astype(BF16), sum_im.astype(BF16)], 1))
        inter = dot_nt(jnp.concatenate(blocks, 0), full[...])
        start = pl.multiple_of(group * 4 * rows, 4 * rows)
        tall[pl.ds(start, 4 * rows), :] = inter[:, 0:grid].astype(BF16)
        tall[pl.ds(grid + start, 4 * rows), :] = inter[:, grid:].astype(BF16)
        return carry

    lax.fori_loop(0, groups, first_period, 0)
    diff[...] = dot_nn(full[...], tall[...])

    def near_in(other, carry):
        arrive(near_recv, other, near_rs)
        return carry

    lax.fori_loop(0, tiles, near_in, 0)
    for pair in range(tiles // 2):
        real_part, imag_part = pair_of(near_recv, pair)
        top = slice(pair * parts, (pair + 1) * parts)
        low = slice(grid + pair * parts, grid + (pair + 1) * parts)
        tall[top, :] = (diff[top, :] + c1r * real_part - c1i * imag_part).astype(BF16)
        tall[low, :] = (diff[low, :] + c1r * imag_part + c1i * real_part).astype(BF16)

    def chunk_out(step, carry):
        chunk = lax.rem(t // 4 + turn(step, groups), groups)
        start = pl.multiple_of(chunk * 4 * rows, 4 * rows)
        inter_re = dot_nn(full[pl.ds(start, 4 * rows), :], tall[...])
        inter_im = dot_nn(full[pl.ds(start + grid, 4 * rows), :], tall[...])
        for i in range(4):
            to = 4 * chunk + i
            back_send[to] = jnp.concatenate(
                [inter_re[i * rows : (i + 1) * rows], inter_im[i * rows : (i + 1) * rows]], 0
            ).astype(BF16)

            @pl.when(t < tiles - 1)
            def _():
                deliver(back_send.at[to], back_recv, to, back_ss, back_rs, t + 1)

            @pl.when(t == tiles - 1)
            def _():
                pltpu.make_async_remote_copy(
                    src_ref=back_send.at[to],
                    dst_ref=back_recv.at[0],
                    send_sem=back_ss.at[to],
                    recv_sem=back_rs.at[0],
                    device_id=(lax.rem(c + 1, cuts), to),
                    device_id_type=MESH,
                ).start()

        return carry

    lax.fori_loop(0, groups, chunk_out, 0)

    def last_period(step, carry):
        group = lax.rem(t // 4 + turn(step, groups), groups)
        blocks = []
        for i in range(4):
            arrive(back_recv, 4 * group + i, back_rs)
        for i in range(2):
            real_part, imag_part = pair_of(back_recv, 2 * group + i)
            blocks.append(jnp.concatenate([real_part.astype(BF16), imag_part.astype(BF16)], 1))
        result = dot_nt(jnp.concatenate(blocks, 0), full[...])
        for i in range(4):
            slot = 4 * group + i
            for q in range(columns):
                for part in range(2):
                    at = part * grid + q * LANES
                    field_v[q, pl.ds(part * slots + slot, rows, stride=2 * slots), :] = result[
                        i * rows : (i + 1) * rows, at : at + LANES
                    ]
        return carry

    lax.fori_loop(0, groups, last_period, 0)
    stores = [
        pltpu.make_async_copy(
            field_v.at[q, pl.ds(0, field_rows)], out_hbm.at[:, pl.ds(q * LANES, LANES)], local_sem.at[8 + q]
        )
        for q in range(columns)
    ]
    for store in stores:
        store.start()

    def sent_theta(step, carry):
        other = lax.rem(c + step, cuts)
        theta_copy(other, other, other).wait_send()
        return carry

    lax.fori_loop(1, cuts, sent_theta, 0)

    def leave(to, send):
        block_copy(back_send.at[0], back_recv.at[0], to, send.at[to], back_rs.at[0]).wait_send()

    def sent(step, carry):
        other = lax.rem(t + step, tiles)
        leave(other, field_ss)
        leave(other, far_ss)
        leave(other, back_ss)

        @pl.when(lax.rem(other, 2) == 1)
        def _():
            leave(other, near_ss)

        return carry

    lax.fori_loop(1, tiles, sent, 0)

    @pl.when(odd)
    def _():
        def sent_twin(other, carry):
            leave(other, twin_ss)
            return carry

        lax.fori_loop(0, tiles, sent_twin, 0)

    hop_copy(0, field_send.at[0], field_hop.at[0]).wait_send()
    hop_copy(1, source_send.at[0], source_hop.at[0]).wait_send()

    @pl.when(t == tiles - 1)
    def _():
        leave(t, back_ss)

    for store in stores:
        store.wait()


def on_device(cuts, tiles, field_in, propagator, theta, cell_x, cell_y, src_dev, src_slot, weights, coupling):
    grid = propagator.shape[1]
    rows = grid // tiles
    slots, share = theta.shape
    slices = src_dev.shape[0]
    hbm = pl.BlockSpec(memory_space=pltpu.HBM)
    block = (2 * rows, grid)
    blocks = pltpu.VMEM((tiles,) + block, BF16)
    dma = pltpu.SemaphoreType.DMA
    result = pl.pallas_call(
        functools.partial(section_kernel, cuts, tiles),
        out_shape=jax.ShapeDtypeStruct((rows * 2 * slots, grid), F32),
        in_specs=[hbm] * 9,
        out_specs=hbm,
        scratch_shapes=[
            pltpu.VMEM((slots, share), F32),
            pltpu.VMEM((2, slices), jnp.int32),
            pltpu.VMEM((2, slices), jnp.int32),
            pltpu.SMEM((2, slices), F32),
            pltpu.SMEM((2, 2), F32),
            pltpu.VMEM((grid // LANES, (rows + 1) * 2 * slots, LANES), F32),
            pltpu.VMEM((2, grid, grid), BF16),
            pltpu.VMEM((slots, 2, share), jnp.int32),
            pltpu.VMEM((slots, 2, share), jnp.int32),
            pltpu.VMEM((16, slices), jnp.int32),
            pltpu.SMEM((16, slices), jnp.int32),
            pltpu.VMEM((slots, share // LANES, LANES), F32),
            pltpu.VMEM((cuts * CAP, share // LANES, LANES), jnp.int16),
            pltpu.VMEM((cuts * CAP, share // LANES, LANES), jnp.int16),
            pltpu.VMEM((2 * slots, 16, share), BF16),
            pltpu.VMEM((2 * slots, 16, share), BF16),
            pltpu.VMEM((2 * grid, 2 * grid), BF16),
            blocks,
            blocks,
            pltpu.VMEM((1,) + block, BF16),
            pltpu.VMEM((1,) + block, BF16),
            blocks,
            blocks,
            blocks,
            pltpu.VMEM((2 * grid, grid), BF16),
            pltpu.VMEM((2 * grid, grid), F32),
            blocks,
            blocks,
            dma((12,)),
            dma((cuts,)),
            dma((cuts,)),
            dma((tiles,)),
            dma((tiles,)),
            dma((tiles,)),
            dma((tiles,)),
            dma((tiles,)),
            dma((tiles,)),
            dma((tiles,)),
            dma((2,)),
            dma((2,)),
            dma((tiles,)),
            dma((tiles,)),
        ],
        compiler_params=pltpu.CompilerParams(
            collective_id=0, has_side_effects=True, vmem_limit_bytes=64 * 1024 * 1024
        ),
    )(
        theta,
        src_dev.T,
        src_slot.T,
        weights.T,
        coupling,
        field_in.reshape(rows * 2 * slots, grid),
        propagator,
        cell_x,
        cell_y,
    )
    return result.reshape(rows, 2, slots, grid)


def solution(mesh):
    in_specs = (
        P("tile", None, "cuts", None),
        P(),
        P("cuts", "tile"),
        P("cuts", None, "tile"),
        P("cuts", None, "tile"),
        P(),
        P(),
        P(),
        P(),
    )
    out_specs = P("tile", None, "cuts", None)
    run = functools.partial(on_device, mesh.shape["cuts"], mesh.shape["tile"])
    return jax.shard_map(run, mesh=mesh, in_specs=in_specs, out_specs=out_specs, check_vma=False)
```

```python
import functools
import math

import jax
import jax.numpy as jnp
from jax import lax
from jax.experimental import pallas as pl
from jax.experimental.pallas import tpu as pltpu
from jax.sharding import PartitionSpec as P

HARM = 5
CAP = 4
LANES = 128
MESH = pl.DeviceIdType.MESH
SIN_PI = (
    3.141592502593994,
    -5.1677069664001465,
    2.5500311851501465,
    -0.5980440974235535,
    0.07721816748380661,
)
F32 = jnp.float32
BF16 = jnp.bfloat16


def sin_pi(fraction):
    square = fraction * fraction
    total = jnp.full_like(square, SIN_PI[4])
    for coefficient in SIN_PI[3::-1]:
        total = total * square + coefficient
    return total * fraction


def turn(step, count):
    return count // 2 + (1 - 2 * lax.rem(step, 2)) * ((step + 1) // 2)


def dot_nn(left, right):
    return lax.dot_general(left, right, (((1,), (0,)), ((), ())), preferred_element_type=F32)


def dot_nt(left, right):
    return lax.dot_general(left, right, (((1,), (1,)), ((), ())), preferred_element_type=F32)


def rank_tables(me, dev, slot, cuts, tables):
    slices = dev.shape[1]
    per_block = slices // cuts
    source = lax.broadcasted_iota(jnp.int32, (cuts, slices), 0)
    low = lax.broadcasted_iota(jnp.int32, (slices, slices), 0)
    high = lax.broadcasted_iota(jnp.int32, (slices, slices), 1)
    same = low // per_block == high // per_block
    block = jnp.where(same, 1.0, 0.0).astype(BF16)
    before = jnp.where(same & (low < high), 1.0, 0.0).astype(BF16)
    hit0 = jnp.where(dev[0:1] == source, 1.0, 0.0)
    hit1 = jnp.where(dev[1:2] == source, 1.0, 0.0)
    rank0 = dot_nn(hit0.astype(BF16), before)
    rank1 = dot_nn(hit1.astype(BF16), before) + dot_nn(hit0.astype(BF16), block)
    rank0 = jnp.sum(hit0 * rank0, axis=0, keepdims=True)
    rank1 = jnp.sum(hit1 * rank1, axis=0, keepdims=True)
    arrival0 = dev[0:1] * CAP + rank0.astype(jnp.int32)
    arrival1 = dev[1:2] * CAP + rank1.astype(jnp.int32)
    tables[0:1, :] = arrival0
    tables[1:2, :] = arrival1
    wanted = lax.broadcasted_iota(jnp.int32, (8, slices), 0).astype(F32)
    mine0 = (dev[0:1] == me) & (rank0 == wanted)
    mine1 = (dev[1:2] == me) & (rank1 == wanted)
    slots = jnp.where(mine0, slot[0:1].astype(F32), 0.0) + jnp.where(mine1, slot[1:2].astype(F32), 0.0)
    place = lax.broadcasted_iota(jnp.int32, (slices, LANES), 0) // per_block
    column = lax.broadcasted_iota(jnp.int32, (slices, LANES), 1)
    chosen = dot_nn(slots.astype(BF16), jnp.where(place == column, 1.0, 0.0).astype(BF16))
    tables[8:16, 0:LANES] = chosen.astype(jnp.int32)


def section_kernel(
    cuts,
    tiles,
    theta_hbm,
    dev_hbm,
    slot_hbm,
    weight_hbm,
    coupling_hbm,
    field_hbm,
    prop_hbm,
    cellx_hbm,
    celly_hbm,
    wide_ref,
    prop_v,
    theta_ref,
    dev_ref,
    slot_ref,
    weight_ref,
    coupling_ref,
    field_v,
    cellx_v,
    celly_v,
    tables_v,
    tables_s,
    phase_v,
    outgoing,
    arrived,
    row_code,
    col_code,
    full,
    field_send,
    source_send,
    field_hop,
    source_hop,
    field_recv,
    near_recv,
    far_recv,
    tall,
    diff,
    back_send,
    back_recv,
    local_sem,
    theta_ss,
    theta_rs,
    field_ss,
    field_rs,
    near_ss,
    near_rs,
    far_ss,
    far_rs,
    twin_ss,
    hop_ss,
    hop_rs,
    back_ss,
    back_rs,
):
    c = lax.axis_index("cuts")
    t = lax.axis_index("tile")
    slots = theta_ref.shape[0]
    share = theta_ref.shape[1]
    pieces = share // LANES
    grid = prop_v.shape[1]
    rows = grid // tiles
    parts = 2 * rows
    columns = grid // LANES
    groups = tiles // 4
    field_rows = 2 * slots * rows

    first = [
        pltpu.make_async_copy(dev_hbm, dev_ref, local_sem.at[0]),
        pltpu.make_async_copy(slot_hbm, slot_ref, local_sem.at[1]),
        pltpu.make_async_copy(theta_hbm, theta_ref, local_sem.at[2]),
        pltpu.make_async_copy(weight_hbm, weight_ref, local_sem.at[3]),
        pltpu.make_async_copy(coupling_hbm, coupling_ref, local_sem.at[4]),
        pltpu.make_async_copy(cellx_hbm, cellx_v, local_sem.at[5]),
        pltpu.make_async_copy(celly_hbm, celly_v, local_sem.at[6]),
        pltpu.make_async_copy(prop_hbm, prop_v, local_sem.at[7]),
    ]
    field_loads = [
        pltpu.make_async_copy(
            field_hbm.at[:, pl.ds(q * LANES, LANES)], field_v.at[q, pl.ds(0, field_rows)], local_sem.at[8 + q]
        )
        for q in range(columns)
    ]
    for load in first + field_loads:
        load.start()
    barrier = pltpu.get_barrier_semaphore()

    def greet_cut(step, carry):
        pl.semaphore_signal(barrier, inc=1, device_id=(lax.rem(c + step, cuts), t), device_id_type=MESH)
        return carry

    def greet_tile(step, carry):
        pl.semaphore_signal(barrier, inc=1, device_id=(c, lax.rem(t + step, tiles)), device_id_type=MESH)
        return carry

    lax.fori_loop(1, cuts, greet_cut, 0)
    lax.fori_loop(1, tiles, greet_tile, 0)
    pl.semaphore_signal(
        barrier, inc=1, device_id=(lax.rem(c + cuts - 1, cuts), tiles - 1), device_id_type=MESH
    )

    first[0].wait()
    first[1].wait()
    rank_tables(c, dev_ref[...], slot_ref[...], cuts, tables_v)
    to_scalar = pltpu.make_async_copy(tables_v, tables_s, local_sem.at[11])
    to_scalar.start()

    first[2].wait()
    turns = theta_ref[...] * (HARM / (2.0 * math.pi))
    turns = turns - jnp.floor(turns + 0.5)
    turns = jnp.minimum(jnp.floor(turns * 65536.0 + 0.5), 32767.0)
    for piece in range(pieces):
        phase_v[:, piece, :] = turns[:, piece * LANES : (piece + 1) * LANES]
    def hop_copy(which, src, dst):
        return pltpu.make_async_remote_copy(
            src_ref=src,
            dst_ref=dst,
            send_sem=hop_ss.at[which],
            recv_sem=hop_rs.at[which],
            device_id=(lax.rem(c + 1, cuts), t),
            device_id_type=MESH,
        )

    def block_copy(src, dst, to, send, recv):
        return pltpu.make_async_remote_copy(
            src_ref=src, dst_ref=dst, send_sem=send, recv_sem=recv, device_id=(c, to), device_id_type=MESH
        )

    def deliver(src, dst, to, send, recv, place=t):
        @pl.when(to == t)
        def _():
            pltpu.make_async_copy(src, dst.at[place], recv.at[place]).start()

        @pl.when(to != t)
        def _():
            block_copy(src, dst.at[place], to, send.at[to], recv.at[place]).start()

    def arrive(dst, other, recv):
        block_copy(back_send.at[0], dst.at[other], other, back_ss.at[0], recv.at[other]).wait_recv()

    def stage_field(slot):
        pieces_re = [field_v[q, pl.ds(slot, rows, stride=2 * slots), :] for q in range(columns)]
        pieces_im = [field_v[q, pl.ds(slot + slots, rows, stride=2 * slots), :] for q in range(columns)]
        field_send[slot] = jnp.concatenate(
            [jnp.concatenate(pieces_re, 1), jnp.concatenate(pieces_im, 1)], 0
        ).astype(BF16)

    for load in field_loads:
        load.wait()
    stage_field(slots - 1)
    pl.semaphore_wait(barrier, cuts + tiles - 2 + tiles * (t // (tiles - 1)))
    hop_copy(0, field_send.at[slots - 1], field_hop.at[0]).start()
    to_scalar.wait()

    def pick(block, carry):
        for rank in range(CAP):
            chosen = jnp.clip(tables_s[8 + rank, block], 0, slots - 1)
            outgoing[block * CAP + rank] = phase_v[chosen].astype(jnp.int32).astype(jnp.int16)
        return carry

    lax.fori_loop(0, cuts, pick, 0)

    def theta_copy(to, slot_of, sem_of):
        return pltpu.make_async_remote_copy(
            src_ref=outgoing.at[pl.ds(to * CAP, CAP)],
            dst_ref=arrived.at[pl.ds(slot_of * CAP, CAP)],
            send_sem=theta_ss.at[to],
            recv_sem=theta_rs.at[sem_of],
            device_id=(to, t),
            device_id_type=MESH,
        )

    def theta_start(step, carry):
        theta_copy(lax.rem(c + step, cuts), c, c).start()
        return carry

    lax.fori_loop(1, cuts, theta_start, 0)
    own_theta = pltpu.make_async_copy(
        outgoing.at[pl.ds(c * CAP, CAP)], arrived.at[pl.ds(c * CAP, CAP)], theta_rs.at[c]
    )
    own_theta.start()

    def one_field(step, carry):
        slot = lax.rem(t + turn(step, slots), slots)

        @pl.when(slot < slots - 1)
        def _():
            stage_field(slot)
            deliver(field_send.at[slot], field_recv, slot + 1, field_ss, field_rs)

        return carry

    lax.fori_loop(0, slots, one_field, 0)
    hop_copy(0, field_send.at[0], field_hop.at[0]).wait_recv()
    deliver(field_hop.at[0], field_recv, 0, field_ss, field_rs)

    for load in first[3:]:
        load.wait()

    def codes(index, carry):
        cell_x = cellx_v[index]
        cell_y = celly_v[index]
        code = (cell_y // LANES) * rows + cell_x
        column = cell_y % LANES
        for k in range(2):
            row_code[2 * index + k] = jnp.broadcast_to(code[k : k + 1].astype(F32), (16, share)).astype(BF16)
            col_code[2 * index + k] = jnp.broadcast_to(column[k : k + 1].astype(F32), (16, share)).astype(BF16)
        return carry

    lax.fori_loop(0, slots, codes, 0)
    full[0:grid, 0:grid] = prop_v[0]
    full[0:grid, grid:] = -prop_v[1]
    full[grid:, 0:grid] = prop_v[1]
    full[grid:, grid:] = prop_v[0]

    own_theta.wait()

    def theta_end(step, carry):
        other = lax.rem(c + step, cuts)
        theta_copy(other, other, other).wait_recv()
        return carry

    lax.fori_loop(1, cuts, theta_end, 0)

    width = 4 * LANES
    subs = lax.broadcasted_iota(jnp.int32, (16, width), 0)
    levels = [(subs + 16 * level).astype(F32).astype(BF16) for level in range(8)]
    one = jnp.ones((16, width), BF16)
    zero = jnp.zeros((16, width), BF16)
    c0r, c0i = coupling_ref[0, 0], coupling_ref[0, 1]
    c1r, c1i = coupling_ref[1, 0], coupling_ref[1, 1]

    def deposit(slot):
        total = None
        for k in range(2):
            entry = c * slots + slot
            row = jnp.clip(tables_s[k, entry], 0, cuts * CAP - 1)
            weight = weight_ref[k, entry]
            phase = arrived[row].astype(jnp.int32).astype(F32) * (1.0 / 32768.0)
            cosine = sin_pi(0.5 - jnp.abs(phase))
            sine = sin_pi(jnp.maximum(jnp.minimum(phase, 1.0 - phase), -1.0 - phase))
            value_re = weight * cosine
            value_im = weight * sine
            index = 2 * slot + k
            for group in range(pieces // 4):
                lanes = slice(group * width, (group + 1) * width)
                column = col_code[index, :, lanes]
                code = row_code[index, :, lanes]
                spread_re = jnp.concatenate(
                    [jnp.broadcast_to(value_re[4 * group + i : 4 * group + i + 1], (16, LANES)) for i in range(4)], 1
                ).astype(BF16)
                spread_im = jnp.concatenate(
                    [jnp.broadcast_to(value_im[4 * group + i : 4 * group + i + 1], (16, LANES)) for i in range(4)], 1
                ).astype(BF16)
                hits = [code == level for level in levels[:5]]
                left = jnp.concatenate(
                    [jnp.where(hit, spread_re, zero) for hit in hits]
                    + [jnp.where(hit, spread_im, zero) for hit in hits],
                    0,
                )
                right = jnp.concatenate([jnp.where(column == level, one, zero) for level in levels], 0)
                product = dot_nt(left, right)
                total = product if total is None else total + product
        real_part = jnp.concatenate([total[i * rows : (i + 1) * rows] for i in range(3)], 1)
        imag_part = jnp.concatenate([total[80 + i * rows : 80 + (i + 1) * rows] for i in range(3)], 1)
        source_send[slot] = jnp.concatenate([real_part, imag_part], 0).astype(BF16)

    deposit(slots - 1)
    hop_copy(1, source_send.at[slots - 1], source_hop.at[0]).start()
    deliver(source_send.at[slots - 1], near_recv, slots - 1, near_ss, near_rs)

    def one_slot(step, carry):
        slot = lax.rem(t + turn(step, slots), slots)

        @pl.when(slot < slots - 1)
        def _():
            deposit(slot)
            deliver(source_send.at[slot], far_recv, slot + 1, far_ss, far_rs)

        @pl.when((lax.rem(slot, 2) == 1) & (slot < slots - 1))
        def _():
            deliver(source_send.at[slot], near_recv, slot, near_ss, near_rs)

        @pl.when(step == 4)
        def _():
            hop_copy(1, source_send.at[0], source_hop.at[0]).wait_recv()
            deliver(source_hop.at[0], far_recv, 0, far_ss, far_rs)

        return carry

    lax.fori_loop(0, slots, one_slot, 0)

    def field_in(other, carry):
        arrive(field_recv, other, field_rs)
        return carry

    lax.fori_loop(0, tiles, field_in, 0)
    odd = lax.rem(t, 2) == 1

    def pair_of(ref, pair):
        first = ref[2 * pair].astype(F32)
        second = ref[2 * pair + 1].astype(F32)
        real_part = jnp.concatenate([first[:rows], second[:rows]], 0)
        imag_part = jnp.concatenate([first[rows:], second[rows:]], 0)
        return real_part, imag_part

    def first_period(step, carry):
        group = lax.rem(t // 4 + turn(step, groups), groups)
        for i in range(4):
            other = 4 * group + i
            arrive(far_recv, other, far_rs)

            @pl.when(odd)
            def _():
                block_copy(
                    far_recv.at[other], near_recv.at[other], t - 1, twin_ss.at[other], near_rs.at[other]
                ).start()

        blocks = []
        for i in range(2):
            field_re, field_im = pair_of(field_recv, 2 * group + i)
            source_re, source_im = pair_of(far_recv, 2 * group + i)
            sum_re = field_re + c0r * source_re - c0i * source_im
            sum_im = field_im + c0r * source_im + c0i * source_re
            blocks.append(jnp.concatenate([sum_re.astype(BF16), sum_im.astype(BF16)], 1))
        inter = dot_nt(jnp.concatenate(blocks, 0), full[...])
        start = pl.multiple_of(group * 4 * rows, 4 * rows)
        tall[pl.ds(start, 4 * rows), :] = inter[:, 0:grid].astype(BF16)
        tall[pl.ds(grid + start, 4 * rows), :] = inter[:, grid:].astype(BF16)
        return carry

    lax.fori_loop(0, groups, first_period, 0)
    diff[...] = dot_nn(full[...], tall[...])

    def near_in(other, carry):
        arrive(near_recv, other, near_rs)
        return carry

    lax.fori_loop(0, tiles, near_in, 0)
    for pair in range(tiles // 2):
        real_part, imag_part = pair_of(near_recv, pair)
        top = slice(pair * parts, (pair + 1) * parts)
        low = slice(grid + pair * parts, grid + (pair + 1) * parts)
        tall[top, :] = (diff[top, :] + c1r * real_part - c1i * imag_part).astype(BF16)
        tall[low, :] = (diff[low, :] + c1r * imag_part + c1i * real_part).astype(BF16)

    def chunk_out(step, carry):
        chunk = lax.rem(t // 4 + turn(step, groups), groups)
        start = pl.multiple_of(chunk * 4 * rows, 4 * rows)
        inter_re = dot_nn(full[pl.ds(start, 4 * rows), :], tall[...])
        inter_im = dot_nn(full[pl.ds(start + grid, 4 * rows), :], tall[...])
        for i in range(4):
            to = 4 * chunk + i
            back_send[to] = jnp.concatenate(
                [inter_re[i * rows : (i + 1) * rows], inter_im[i * rows : (i + 1) * rows]], 0
            ).astype(BF16)

            @pl.when(t < tiles - 1)
            def _():
                deliver(back_send.at[to], back_recv, to, back_ss, back_rs, t + 1)

            @pl.when(t == tiles - 1)
            def _():
                pltpu.make_async_remote_copy(
                    src_ref=back_send.at[to],
                    dst_ref=back_recv.at[0],
                    send_sem=back_ss.at[to],
                    recv_sem=back_rs.at[0],
                    device_id=(lax.rem(c + 1, cuts), to),
                    device_id_type=MESH,
                ).start()

        return carry

    lax.fori_loop(0, groups, chunk_out, 0)

    def gather(step, carry):
        group = lax.rem(t // 4 + turn(step, groups), groups)
        for i in range(4):
            slot = 4 * group + i
            arrive(back_recv, slot, back_rs)
            block = back_recv[slot].astype(F32)
            for q in range(columns):
                for part in range(2):
                    field_v[q, pl.ds(part * grid + slot, rows, stride=slots), :] = block[
                        part * rows : (part + 1) * rows, q * LANES : (q + 1) * LANES
                    ]
        return carry

    lax.fori_loop(0, groups, gather, 0)
    for q in range(columns):
        for part in range(2):
            at = part * grid + q * LANES
            wide_ref[:, at : at + LANES] = field_v[q, part * grid : (part + 1) * grid, :].astype(BF16)

    def sent_theta(step, carry):
        other = lax.rem(c + step, cuts)
        theta_copy(other, other, other).wait_send()
        return carry

    lax.fori_loop(1, cuts, sent_theta, 0)

    def leave(to, send):
        block_copy(back_send.at[0], back_recv.at[0], to, send.at[to], back_rs.at[0]).wait_send()

    def sent(step, carry):
        other = lax.rem(t + step, tiles)
        leave(other, field_ss)
        leave(other, far_ss)
        leave(other, back_ss)

        @pl.when(lax.rem(other, 2) == 1)
        def _():
            leave(other, near_ss)

        return carry

    lax.fori_loop(1, tiles, sent, 0)

    @pl.when(odd)
    def _():
        def sent_twin(other, carry):
            leave(other, twin_ss)
            return carry

        lax.fori_loop(0, tiles, sent_twin, 0)

    hop_copy(0, field_send.at[0], field_hop.at[0]).wait_send()
    hop_copy(1, source_send.at[0], source_hop.at[0]).wait_send()

    @pl.when(t == tiles - 1)
    def _():
        leave(t, back_ss)


def final_kernel(wide_ref, prop_ref, out_ref):
    grid = prop_ref.shape[1]
    rows, _, slots, _ = out_ref.shape
    real_part = wide_ref[:, 0:grid]
    imag_part = wide_ref[:, grid:]
    out_re = dot_nt(real_part, prop_ref[0]) - dot_nt(imag_part, prop_ref[1])
    out_ref[:, 0] = out_re.reshape(rows, slots, grid)
    out_im = dot_nt(imag_part, prop_ref[0]) + dot_nt(real_part, prop_ref[1])
    out_ref[:, 1] = out_im.reshape(rows, slots, grid)


def on_device(cuts, tiles, field_in, propagator, theta, cell_x, cell_y, src_dev, src_slot, weights, coupling):
    grid = propagator.shape[1]
    rows = grid // tiles
    slots, share = theta.shape
    slices = src_dev.shape[0]
    hbm = pl.BlockSpec(memory_space=pltpu.HBM)
    vmem = pl.BlockSpec(memory_space=pltpu.VMEM)
    block = (2 * rows, grid)
    blocks = pltpu.VMEM((tiles,) + block, BF16)
    dma = pltpu.SemaphoreType.DMA
    operands = (
        theta,
        src_dev.T,
        src_slot.T,
        weights.T,
        coupling,
        field_in.reshape(rows * 2 * slots, grid),
        propagator,
        cell_x,
        cell_y,
    )
    operands = [pltpu.with_memory_space_constraint(value, pltpu.HBM) for value in operands]
    wide, prop = pl.pallas_call(
        functools.partial(section_kernel, cuts, tiles),
        out_shape=[pltpu.VMEM((grid, 2 * grid), BF16), pltpu.VMEM((2, grid, grid), BF16)],
        in_specs=[hbm] * 9,
        out_specs=[vmem, vmem],
        scratch_shapes=[
            pltpu.VMEM((slots, share), F32),
            pltpu.VMEM((2, slices), jnp.int32),
            pltpu.VMEM((2, slices), jnp.int32),
            pltpu.SMEM((2, slices), F32),
            pltpu.SMEM((2, 2), F32),
            pltpu.VMEM((grid // LANES, (rows + 1) * 2 * slots, LANES), F32),
            pltpu.VMEM((slots, 2, share), jnp.int32),
            pltpu.VMEM((slots, 2, share), jnp.int32),
            pltpu.VMEM((16, slices), jnp.int32),
            pltpu.SMEM((16, slices), jnp.int32),
            pltpu.VMEM((slots, share // LANES, LANES), F32),
            pltpu.VMEM((cuts * CAP, share // LANES, LANES), jnp.int16),
            pltpu.VMEM((cuts * CAP, share // LANES, LANES), jnp.int16),
            pltpu.VMEM((2 * slots, 16, share), BF16),
            pltpu.VMEM((2 * slots, 16, share), BF16),
            pltpu.VMEM((2 * grid, 2 * grid), BF16),
            blocks,
            blocks,
            pltpu.VMEM((1,) + block, BF16),
            pltpu.VMEM((1,) + block, BF16),
            blocks,
            blocks,
            blocks,
            pltpu.VMEM((2 * grid, grid), BF16),
            pltpu.VMEM((2 * grid, grid), F32),
            blocks,
            blocks,
            dma((12,)),
            dma((cuts,)),
            dma((cuts,)),
            dma((tiles,)),
            dma((tiles,)),
            dma((tiles,)),
            dma((tiles,)),
            dma((tiles,)),
            dma((tiles,)),
            dma((tiles,)),
            dma((2,)),
            dma((2,)),
            dma((tiles,)),
            dma((tiles,)),
        ],
        compiler_params=pltpu.CompilerParams(
            collective_id=0, has_side_effects=True, vmem_limit_bytes=48 * 1024 * 1024
        ),
    )(*operands)
    return pl.pallas_call(
        final_kernel,
        out_shape=jax.ShapeDtypeStruct((rows, 2, slots, grid), F32),
        in_specs=[vmem, vmem],
        out_specs=vmem,
        compiler_params=pltpu.CompilerParams(vmem_limit_bytes=32 * 1024 * 1024),
    )(wide, prop)


def solution(mesh):
    in_specs = (
        P("tile", None, "cuts", None),
        P(),
        P("cuts", "tile"),
        P("cuts", None, "tile"),
        P("cuts", None, "tile"),
        P(),
        P(),
        P(),
        P(),
    )
    out_specs = P("tile", None, "cuts", None)
    run = functools.partial(on_device, mesh.shape["cuts"], mesh.shape["tile"])
    return jax.shard_map(run, mesh=mesh, in_specs=in_specs, out_specs=out_specs, check_vma=False)
```

```python
import functools
import math

import jax
import jax.numpy as jnp
from jax import lax
from jax.experimental import pallas as pl
from jax.experimental.pallas import tpu as pltpu
from jax.sharding import PartitionSpec as P

HARM = 5
CAP = 4
LANES = 128
MESH = pl.DeviceIdType.MESH
SIN_PI = (
    3.141592502593994,
    -5.1677069664001465,
    2.5500311851501465,
    -0.5980440974235535,
    0.07721816748380661,
)
F32 = jnp.float32
BF16 = jnp.bfloat16


def sin_pi(fraction):
    square = fraction * fraction
    total = jnp.full_like(square, SIN_PI[4])
    for coefficient in SIN_PI[3::-1]:
        total = total * square + coefficient
    return total * fraction


def turn(step, count):
    return count // 2 + (1 - 2 * lax.rem(step, 2)) * ((step + 1) // 2)


def dot_nn(left, right):
    return lax.dot_general(left, right, (((1,), (0,)), ((), ())), preferred_element_type=F32)


def dot_nt(left, right):
    return lax.dot_general(left, right, (((1,), (1,)), ((), ())), preferred_element_type=F32)


def rank_tables(me, dev, slot, cuts, tables):
    slices = dev.shape[1]
    per_block = slices // cuts
    source = lax.broadcasted_iota(jnp.int32, (cuts, slices), 0)
    low = lax.broadcasted_iota(jnp.int32, (slices, slices), 0)
    high = lax.broadcasted_iota(jnp.int32, (slices, slices), 1)
    same = low // per_block == high // per_block
    block = jnp.where(same, 1.0, 0.0).astype(BF16)
    before = jnp.where(same & (low < high), 1.0, 0.0).astype(BF16)
    hit0 = jnp.where(dev[0:1] == source, 1.0, 0.0)
    hit1 = jnp.where(dev[1:2] == source, 1.0, 0.0)
    rank0 = dot_nn(hit0.astype(BF16), before)
    rank1 = dot_nn(hit1.astype(BF16), before) + dot_nn(hit0.astype(BF16), block)
    rank0 = jnp.sum(hit0 * rank0, axis=0, keepdims=True)
    rank1 = jnp.sum(hit1 * rank1, axis=0, keepdims=True)
    arrival0 = dev[0:1] * CAP + rank0.astype(jnp.int32)
    arrival1 = dev[1:2] * CAP + rank1.astype(jnp.int32)
    tables[0:1, :] = arrival0
    tables[1:2, :] = arrival1
    wanted = lax.broadcasted_iota(jnp.int32, (8, slices), 0).astype(F32)
    mine0 = (dev[0:1] == me) & (rank0 == wanted)
    mine1 = (dev[1:2] == me) & (rank1 == wanted)
    slots = jnp.where(mine0, slot[0:1].astype(F32), 0.0) + jnp.where(mine1, slot[1:2].astype(F32), 0.0)
    place = lax.broadcasted_iota(jnp.int32, (slices, LANES), 0) // per_block
    column = lax.broadcasted_iota(jnp.int32, (slices, LANES), 1)
    chosen = dot_nn(slots.astype(BF16), jnp.where(place == column, 1.0, 0.0).astype(BF16))
    tables[8:16, 0:LANES] = chosen.astype(jnp.int32)


def section_kernel(
    cuts,
    tiles,
    theta_hbm,
    dev_hbm,
    slot_hbm,
    weight_hbm,
    coupling_hbm,
    field_hbm,
    prop_hbm,
    cellx_hbm,
    celly_hbm,
    wide_ref,
    prop_v,
    theta_ref,
    dev_ref,
    slot_ref,
    weight_ref,
    coupling_ref,
    field_v,
    cellx_v,
    celly_v,
    tables_v,
    tables_s,
    phase_v,
    outgoing,
    arrived,
    row_code,
    col_code,
    full,
    field_send,
    source_send,
    field_hop,
    source_hop,
    field_recv,
    near_recv,
    far_recv,
    tall,
    diff,
    back_send,
    back_recv,
    local_sem,
    theta_ss,
    theta_rs,
    field_ss,
    field_rs,
    near_ss,
    near_rs,
    far_ss,
    far_rs,
    twin_ss,
    hop_ss,
    hop_rs,
    back_ss,
    back_rs,
):
    c = lax.axis_index("cuts")
    t = lax.axis_index("tile")
    slots = theta_ref.shape[0]
    share = theta_ref.shape[1]
    pieces = share // LANES
    grid = prop_v.shape[1]
    rows = grid // tiles
    parts = 2 * rows
    columns = grid // LANES
    groups = tiles // 4
    field_rows = 2 * slots * rows

    first = [
        pltpu.make_async_copy(dev_hbm, dev_ref, local_sem.at[0]),
        pltpu.make_async_copy(slot_hbm, slot_ref, local_sem.at[1]),
        pltpu.make_async_copy(theta_hbm, theta_ref, local_sem.at[2]),
        pltpu.make_async_copy(weight_hbm, weight_ref, local_sem.at[3]),
        pltpu.make_async_copy(coupling_hbm, coupling_ref, local_sem.at[4]),
        pltpu.make_async_copy(cellx_hbm, cellx_v, local_sem.at[5]),
        pltpu.make_async_copy(celly_hbm, celly_v, local_sem.at[6]),
        pltpu.make_async_copy(prop_hbm, prop_v, local_sem.at[7]),
    ]
    field_loads = [
        pltpu.make_async_copy(
            field_hbm.at[:, pl.ds(q * LANES, LANES)], field_v.at[q, pl.ds(0, field_rows)], local_sem.at[8 + q]
        )
        for q in range(columns)
    ]
    for load in first + field_loads:
        load.start()
    barrier = pltpu.get_barrier_semaphore()

    def greet_cut(step, carry):
        pl.semaphore_signal(barrier, inc=1, device_id=(lax.rem(c + step, cuts), t), device_id_type=MESH)
        return carry

    def greet_tile(step, carry):
        pl.semaphore_signal(barrier, inc=1, device_id=(c, lax.rem(t + step, tiles)), device_id_type=MESH)
        return carry

    lax.fori_loop(1, cuts, greet_cut, 0)
    lax.fori_loop(1, tiles, greet_tile, 0)
    pl.semaphore_signal(
        barrier, inc=1, device_id=(lax.rem(c + cuts - 1, cuts), tiles - 1), device_id_type=MESH
    )

    first[0].wait()
    first[1].wait()
    rank_tables(c, dev_ref[...], slot_ref[...], cuts, tables_v)
    to_scalar = pltpu.make_async_copy(tables_v, tables_s, local_sem.at[11])
    to_scalar.start()

    first[2].wait()
    turns = theta_ref[...] * (HARM / (2.0 * math.pi))
    turns = turns - jnp.floor(turns + 0.5)
    turns = jnp.minimum(jnp.floor(turns * 65536.0 + 0.5), 32767.0)
    for piece in range(pieces):
        phase_v[:, piece, :] = turns[:, piece * LANES : (piece + 1) * LANES]
    def hop_copy(which, src, dst):
        return pltpu.make_async_remote_copy(
            src_ref=src,
            dst_ref=dst,
            send_sem=hop_ss.at[which],
            recv_sem=hop_rs.at[which],
            device_id=(lax.rem(c + 1, cuts), t),
            device_id_type=MESH,
        )

    def block_copy(src, dst, to, send, recv):
        return pltpu.make_async_remote_copy(
            src_ref=src, dst_ref=dst, send_sem=send, recv_sem=recv, device_id=(c, to), device_id_type=MESH
        )

    def deliver(src, dst, to, send, recv, place=t):
        @pl.when(to == t)
        def _():
            pltpu.make_async_copy(src, dst.at[place], recv.at[place]).start()

        @pl.when(to != t)
        def _():
            block_copy(src, dst.at[place], to, send.at[to], recv.at[place]).start()

    def arrive(dst, other, recv):
        block_copy(back_send.at[0], dst.at[other], other, back_ss.at[0], recv.at[other]).wait_recv()

    def stage_field(slot):
        pieces_re = [field_v[q, pl.ds(slot, rows, stride=2 * slots), :] for q in range(columns)]
        pieces_im = [field_v[q, pl.ds(slot + slots, rows, stride=2 * slots), :] for q in range(columns)]
        field_send[slot] = jnp.concatenate(
            [jnp.concatenate(pieces_re, 1), jnp.concatenate(pieces_im, 1)], 0
        ).astype(BF16)

    for load in field_loads:
        load.wait()
    stage_field(slots - 1)
    pl.semaphore_wait(barrier, cuts + tiles - 2 + tiles * (t // (tiles - 1)))
    hop_copy(0, field_send.at[slots - 1], field_hop.at[0]).start()
    to_scalar.wait()

    def pick(block, carry):
        for rank in range(CAP):
            chosen = jnp.clip(tables_s[8 + rank, block], 0, slots - 1)
            outgoing[block * CAP + rank] = phase_v[chosen].astype(jnp.int32).astype(jnp.int16)
        return carry

    lax.fori_loop(0, cuts, pick, 0)

    def theta_copy(to, slot_of, sem_of):
        return pltpu.make_async_remote_copy(
            src_ref=outgoing.at[pl.ds(to * CAP, CAP)],
            dst_ref=arrived.at[pl.ds(slot_of * CAP, CAP)],
            send_sem=theta_ss.at[to],
            recv_sem=theta_rs.at[sem_of],
            device_id=(to, t),
            device_id_type=MESH,
        )

    def theta_start(step, carry):
        theta_copy(lax.rem(c + step, cuts), c, c).start()
        return carry

    lax.fori_loop(1, cuts, theta_start, 0)
    own_theta = pltpu.make_async_copy(
        outgoing.at[pl.ds(c * CAP, CAP)], arrived.at[pl.ds(c * CAP, CAP)], theta_rs.at[c]
    )
    own_theta.start()

    def one_field(step, carry):
        slot = lax.rem(t + turn(step, slots), slots)

        @pl.when(slot < slots - 1)
        def _():
            stage_field(slot)
            deliver(field_send.at[slot], field_recv, slot + 1, field_ss, field_rs)

        return carry

    lax.fori_loop(0, slots, one_field, 0)
    hop_copy(0, field_send.at[0], field_hop.at[0]).wait_recv()
    deliver(field_hop.at[0], field_recv, 0, field_ss, field_rs)

    for load in first[3:]:
        load.wait()

    def codes(index, carry):
        cell_x = cellx_v[index]
        cell_y = celly_v[index]
        code = (cell_y // LANES) * rows + cell_x
        column = cell_y % LANES
        for k in range(2):
            row_code[2 * index + k] = jnp.broadcast_to(code[k : k + 1].astype(F32), (16, share)).astype(BF16)
            col_code[2 * index + k] = jnp.broadcast_to(column[k : k + 1].astype(F32), (16, share)).astype(BF16)
        return carry

    lax.fori_loop(0, slots, codes, 0)
    full[0:grid, 0:grid] = prop_v[0]
    full[0:grid, grid:] = -prop_v[1]
    full[grid:, 0:grid] = prop_v[1]
    full[grid:, grid:] = prop_v[0]

    own_theta.wait()

    def theta_end(step, carry):
        other = lax.rem(c + step, cuts)
        theta_copy(other, other, other).wait_recv()
        return carry

    lax.fori_loop(1, cuts, theta_end, 0)

    width = 4 * LANES
    subs = lax.broadcasted_iota(jnp.int32, (16, width), 0)
    levels = [(subs + 16 * level).astype(F32).astype(BF16) for level in range(8)]
    one = jnp.ones((16, width), BF16)
    zero = jnp.zeros((16, width), BF16)
    c0r, c0i = coupling_ref[0, 0], coupling_ref[0, 1]
    c1r, c1i = coupling_ref[1, 0], coupling_ref[1, 1]

    def deposit(slot):
        total = None
        for k in range(2):
            entry = c * slots + slot
            row = jnp.clip(tables_s[k, entry], 0, cuts * CAP - 1)
            weight = weight_ref[k, entry]
            phase = arrived[row].astype(jnp.int32).astype(F32) * (1.0 / 32768.0)
            cosine = sin_pi(0.5 - jnp.abs(phase))
            sine = sin_pi(jnp.maximum(jnp.minimum(phase, 1.0 - phase), -1.0 - phase))
            value_re = weight * cosine
            value_im = weight * sine
            index = 2 * slot + k
            for group in range(pieces // 4):
                lanes = slice(group * width, (group + 1) * width)
                column = col_code[index, :, lanes]
                code = row_code[index, :, lanes]
                spread_re = jnp.concatenate(
                    [jnp.broadcast_to(value_re[4 * group + i : 4 * group + i + 1], (16, LANES)) for i in range(4)], 1
                ).astype(BF16)
                spread_im = jnp.concatenate(
                    [jnp.broadcast_to(value_im[4 * group + i : 4 * group + i + 1], (16, LANES)) for i in range(4)], 1
                ).astype(BF16)
                hits = [code == level for level in levels[:5]]
                left = jnp.concatenate(
                    [jnp.where(hit, spread_re, zero) for hit in hits]
                    + [jnp.where(hit, spread_im, zero) for hit in hits],
                    0,
                )
                right = jnp.concatenate([jnp.where(column == level, one, zero) for level in levels], 0)
                product = dot_nt(left, right)
                total = product if total is None else total + product
        real_part = jnp.concatenate([total[i * rows : (i + 1) * rows] for i in range(3)], 1)
        imag_part = jnp.concatenate([total[80 + i * rows : 80 + (i + 1) * rows] for i in range(3)], 1)
        source_send[slot] = jnp.concatenate([real_part, imag_part], 0).astype(BF16)

    deposit(slots - 1)
    hop_copy(1, source_send.at[slots - 1], source_hop.at[0]).start()
    deliver(source_send.at[slots - 1], near_recv, slots - 1, near_ss, near_rs)

    def one_slot(step, carry):
        slot = lax.rem(t + turn(step, slots), slots)

        @pl.when(slot < slots - 1)
        def _():
            deposit(slot)
            deliver(source_send.at[slot], far_recv, slot + 1, far_ss, far_rs)

        @pl.when((lax.rem(slot, 2) == 1) & (slot < slots - 1))
        def _():
            deliver(source_send.at[slot], near_recv, slot, near_ss, near_rs)

        @pl.when(step == 12)
        def _():
            hop_copy(1, source_send.at[0], source_hop.at[0]).wait_recv()
            deliver(source_hop.at[0], far_recv, 0, far_ss, far_rs)

        return carry

    lax.fori_loop(0, slots, one_slot, 0)

    def field_in(other, carry):
        arrive(field_recv, other, field_rs)
        return carry

    lax.fori_loop(0, tiles, field_in, 0)
    odd = lax.rem(t, 2) == 1

    def pair_of(ref, pair):
        first = ref[2 * pair].astype(F32)
        second = ref[2 * pair + 1].astype(F32)
        real_part = jnp.concatenate([first[:rows], second[:rows]], 0)
        imag_part = jnp.concatenate([first[rows:], second[rows:]], 0)
        return real_part, imag_part

    def first_period(step, carry):
        group = lax.rem(t // 4 + turn(step, groups), groups)
        for i in range(4):
            other = 4 * group + i
            arrive(far_recv, other, far_rs)

            @pl.when(odd)
            def _():
                block_copy(
                    far_recv.at[other], near_recv.at[other], t - 1, twin_ss.at[other], near_rs.at[other]
                ).start()

        blocks = []
        for i in range(2):
            field_re, field_im = pair_of(field_recv, 2 * group + i)
            source_re, source_im = pair_of(far_recv, 2 * group + i)
            sum_re = field_re + c0r * source_re - c0i * source_im
            sum_im = field_im + c0r * source_im + c0i * source_re
            blocks.append(jnp.concatenate([sum_re.astype(BF16), sum_im.astype(BF16)], 1))
        inter = dot_nt(jnp.concatenate(blocks, 0), full[...])
        start = pl.multiple_of(group * 4 * rows, 4 * rows)
        tall[pl.ds(start, 4 * rows), :] = inter[:, 0:grid].astype(BF16)
        tall[pl.ds(grid + start, 4 * rows), :] = inter[:, grid:].astype(BF16)
        return carry

    lax.fori_loop(0, groups, first_period, 0)
    diff[...] = dot_nn(full[...], tall[...])

    def near_in(other, carry):
        arrive(near_recv, other, near_rs)
        return carry

    lax.fori_loop(0, tiles, near_in, 0)
    for pair in range(tiles // 2):
        real_part, imag_part = pair_of(near_recv, pair)
        top = slice(pair * parts, (pair + 1) * parts)
        low = slice(grid + pair * parts, grid + (pair + 1) * parts)
        tall[top, :] = (diff[top, :] + c1r * real_part - c1i * imag_part).astype(BF16)
        tall[low, :] = (diff[low, :] + c1r * imag_part + c1i * real_part).astype(BF16)

    def chunk_out(step, carry):
        chunk = lax.rem(t // 4 + turn(step, groups), groups)
        start = pl.multiple_of(chunk * 4 * rows, 4 * rows)
        inter_re = dot_nn(full[pl.ds(start, 4 * rows), :], tall[...])
        inter_im = dot_nn(full[pl.ds(start + grid, 4 * rows), :], tall[...])
        for i in range(4):
            to = 4 * chunk + i
            back_send[to] = jnp.concatenate(
                [inter_re[i * rows : (i + 1) * rows], inter_im[i * rows : (i + 1) * rows]], 0
            ).astype(BF16)

            @pl.when(t < tiles - 1)
            def _():
                deliver(back_send.at[to], back_recv, to, back_ss, back_rs, t + 1)

            @pl.when(t == tiles - 1)
            def _():
                pltpu.make_async_remote_copy(
                    src_ref=back_send.at[to],
                    dst_ref=back_recv.at[0],
                    send_sem=back_ss.at[to],
                    recv_sem=back_rs.at[0],
                    device_id=(lax.rem(c + 1, cuts), to),
                    device_id_type=MESH,
                ).start()

        return carry

    lax.fori_loop(0, groups, chunk_out, 0)

    def gather(step, carry):
        group = lax.rem(t // 4 + turn(step, groups), groups)
        for i in range(4):
            slot = 4 * group + i
            arrive(back_recv, slot, back_rs)
            block = back_recv[slot].astype(F32)
            for q in range(columns):
                for part in range(2):
                    field_v[q, pl.ds(part * grid + slot, rows, stride=slots), :] = block[
                        part * rows : (part + 1) * rows, q * LANES : (q + 1) * LANES
                    ]
        return carry

    lax.fori_loop(0, groups, gather, 0)
    for q in range(columns):
        for part in range(2):
            at = part * grid + q * LANES
            wide_ref[:, at : at + LANES] = field_v[q, part * grid : (part + 1) * grid, :].astype(BF16)

    def sent_theta(step, carry):
        other = lax.rem(c + step, cuts)
        theta_copy(other, other, other).wait_send()
        return carry

    lax.fori_loop(1, cuts, sent_theta, 0)

    def leave(to, send):
        block_copy(back_send.at[0], back_recv.at[0], to, send.at[to], back_rs.at[0]).wait_send()

    def sent(step, carry):
        other = lax.rem(t + step, tiles)
        leave(other, field_ss)
        leave(other, far_ss)
        leave(other, back_ss)

        @pl.when(lax.rem(other, 2) == 1)
        def _():
            leave(other, near_ss)

        return carry

    lax.fori_loop(1, tiles, sent, 0)

    @pl.when(odd)
    def _():
        def sent_twin(other, carry):
            leave(other, twin_ss)
            return carry

        lax.fori_loop(0, tiles, sent_twin, 0)

    hop_copy(0, field_send.at[0], field_hop.at[0]).wait_send()
    hop_copy(1, source_send.at[0], source_hop.at[0]).wait_send()

    @pl.when(t == tiles - 1)
    def _():
        leave(t, back_ss)


def final_kernel(wide_ref, prop_ref, out_ref):
    grid = prop_ref.shape[1]
    rows, _, slots, _ = out_ref.shape
    real_part = wide_ref[:, 0:grid]
    imag_part = wide_ref[:, grid:]
    out_re = dot_nt(real_part, prop_ref[0]) - dot_nt(imag_part, prop_ref[1])
    out_ref[:, 0] = out_re.reshape(rows, slots, grid)
    out_im = dot_nt(imag_part, prop_ref[0]) + dot_nt(real_part, prop_ref[1])
    out_ref[:, 1] = out_im.reshape(rows, slots, grid)


def on_device(cuts, tiles, field_in, propagator, theta, cell_x, cell_y, src_dev, src_slot, weights, coupling):
    grid = propagator.shape[1]
    rows = grid // tiles
    slots, share = theta.shape
    slices = src_dev.shape[0]
    hbm = pl.BlockSpec(memory_space=pltpu.HBM)
    vmem = pl.BlockSpec(memory_space=pltpu.VMEM)
    block = (2 * rows, grid)
    blocks = pltpu.VMEM((tiles,) + block, BF16)
    dma = pltpu.SemaphoreType.DMA
    operands = (
        theta,
        src_dev.T,
        src_slot.T,
        weights.T,
        coupling,
        field_in.reshape(rows * 2 * slots, grid),
        propagator,
        cell_x,
        cell_y,
    )
    operands = [pltpu.with_memory_space_constraint(value, pltpu.HBM) for value in operands]
    wide, prop = pl.pallas_call(
        functools.partial(section_kernel, cuts, tiles),
        out_shape=[pltpu.VMEM((grid, 2 * grid), BF16), pltpu.VMEM((2, grid, grid), BF16)],
        in_specs=[hbm] * 9,
        out_specs=[vmem, vmem],
        scratch_shapes=[
            pltpu.VMEM((slots, share), F32),
            pltpu.VMEM((2, slices), jnp.int32),
            pltpu.VMEM((2, slices), jnp.int32),
            pltpu.SMEM((2, slices), F32),
            pltpu.SMEM((2, 2), F32),
            pltpu.VMEM((grid // LANES, (rows + 1) * 2 * slots, LANES), F32),
            pltpu.VMEM((slots, 2, share), jnp.int32),
            pltpu.VMEM((slots, 2, share), jnp.int32),
            pltpu.VMEM((16, slices), jnp.int32),
            pltpu.SMEM((16, slices), jnp.int32),
            pltpu.VMEM((slots, share // LANES, LANES), F32),
            pltpu.VMEM((cuts * CAP, share // LANES, LANES), jnp.int16),
            pltpu.VMEM((cuts * CAP, share // LANES, LANES), jnp.int16),
            pltpu.VMEM((2 * slots, 16, share), BF16),
            pltpu.VMEM((2 * slots, 16, share), BF16),
            pltpu.VMEM((2 * grid, 2 * grid), BF16),
            blocks,
            blocks,
            pltpu.VMEM((1,) + block, BF16),
            pltpu.VMEM((1,) + block, BF16),
            blocks,
            blocks,
            blocks,
            pltpu.VMEM((2 * grid, grid), BF16),
            pltpu.VMEM((2 * grid, grid), F32),
            blocks,
            blocks,
            dma((12,)),
            dma((cuts,)),
            dma((cuts,)),
            dma((tiles,)),
            dma((tiles,)),
            dma((tiles,)),
            dma((tiles,)),
            dma((tiles,)),
            dma((tiles,)),
            dma((tiles,)),
            dma((2,)),
            dma((2,)),
            dma((tiles,)),
            dma((tiles,)),
        ],
        compiler_params=pltpu.CompilerParams(
            collective_id=0, has_side_effects=True, vmem_limit_bytes=48 * 1024 * 1024
        ),
    )(*operands)
    return pl.pallas_call(
        final_kernel,
        out_shape=jax.ShapeDtypeStruct((rows, 2, slots, grid), F32),
        in_specs=[vmem, vmem],
        out_specs=vmem,
        compiler_params=pltpu.CompilerParams(vmem_limit_bytes=32 * 1024 * 1024),
    )(wide, prop)


def solution(mesh):
    in_specs = (
        P("tile", None, "cuts", None),
        P(),
        P("cuts", "tile"),
        P("cuts", None, "tile"),
        P("cuts", None, "tile"),
        P(),
        P(),
        P(),
        P(),
    )
    out_specs = P("tile", None, "cuts", None)
    run = functools.partial(on_device, mesh.shape["cuts"], mesh.shape["tile"])
    return jax.shard_map(run, mesh=mesh, in_specs=in_specs, out_specs=out_specs, check_vma=False)
```

```python
import functools
import math

import jax
import jax.numpy as jnp
from jax import lax
from jax.experimental import pallas as pl
from jax.experimental.pallas import tpu as pltpu
from jax.sharding import PartitionSpec as P

HARM = 5
CAP = 4
LANES = 128
MESH = pl.DeviceIdType.MESH
SIN_PI = (
    3.141592502593994,
    -5.1677069664001465,
    2.5500311851501465,
    -0.5980440974235535,
    0.07721816748380661,
)
F32 = jnp.float32
BF16 = jnp.bfloat16


def sin_pi(fraction):
    square = fraction * fraction
    total = jnp.full_like(square, SIN_PI[4])
    for coefficient in SIN_PI[3::-1]:
        total = total * square + coefficient
    return total * fraction


def turn(step, count):
    return count // 2 + (1 - 2 * lax.rem(step, 2)) * ((step + 1) // 2)


def dot_nn(left, right):
    return lax.dot_general(left, right, (((1,), (0,)), ((), ())), preferred_element_type=F32)


def dot_nt(left, right):
    return lax.dot_general(left, right, (((1,), (1,)), ((), ())), preferred_element_type=F32)


def rank_tables(me, dev, slot, cuts, tables):
    slices = dev.shape[1]
    per_block = slices // cuts
    source = lax.broadcasted_iota(jnp.int32, (cuts, slices), 0)
    low = lax.broadcasted_iota(jnp.int32, (slices, slices), 0)
    high = lax.broadcasted_iota(jnp.int32, (slices, slices), 1)
    same = low // per_block == high // per_block
    block = jnp.where(same, 1.0, 0.0).astype(BF16)
    before = jnp.where(same & (low < high), 1.0, 0.0).astype(BF16)
    hit0 = jnp.where(dev[0:1] == source, 1.0, 0.0)
    hit1 = jnp.where(dev[1:2] == source, 1.0, 0.0)
    rank0 = dot_nn(hit0.astype(BF16), before)
    rank1 = dot_nn(hit1.astype(BF16), before) + dot_nn(hit0.astype(BF16), block)
    rank0 = jnp.sum(hit0 * rank0, axis=0, keepdims=True)
    rank1 = jnp.sum(hit1 * rank1, axis=0, keepdims=True)
    arrival0 = dev[0:1] * CAP + rank0.astype(jnp.int32)
    arrival1 = dev[1:2] * CAP + rank1.astype(jnp.int32)
    tables[0:1, :] = arrival0
    tables[1:2, :] = arrival1
    wanted = lax.broadcasted_iota(jnp.int32, (8, slices), 0).astype(F32)
    mine0 = (dev[0:1] == me) & (rank0 == wanted)
    mine1 = (dev[1:2] == me) & (rank1 == wanted)
    slots = jnp.where(mine0, slot[0:1].astype(F32), 0.0) + jnp.where(mine1, slot[1:2].astype(F32), 0.0)
    place = lax.broadcasted_iota(jnp.int32, (slices, LANES), 0) // per_block
    column = lax.broadcasted_iota(jnp.int32, (slices, LANES), 1)
    chosen = dot_nn(slots.astype(BF16), jnp.where(place == column, 1.0, 0.0).astype(BF16))
    tables[8:16, 0:LANES] = chosen.astype(jnp.int32)


def section_kernel(
    cuts,
    tiles,
    theta_hbm,
    dev_hbm,
    slot_hbm,
    weight_hbm,
    coupling_hbm,
    field_hbm,
    prop_hbm,
    cellx_hbm,
    celly_hbm,
    wide_ref,
    prop_v,
    theta_ref,
    dev_ref,
    slot_ref,
    weight_ref,
    coupling_ref,
    field_v,
    cellx_v,
    celly_v,
    tables_v,
    tables_s,
    phase_v,
    outgoing,
    arrived,
    row_code,
    col_code,
    full,
    field_send,
    source_send,
    field_hop,
    source_hop,
    field_recv,
    near_recv,
    far_recv,
    tall,
    diff,
    back_send,
    back_recv,
    local_sem,
    theta_ss,
    theta_rs,
    field_ss,
    field_rs,
    near_ss,
    near_rs,
    far_ss,
    far_rs,
    twin_ss,
    hop_ss,
    hop_rs,
    back_ss,
    back_rs,
):
    c = lax.axis_index("cuts")
    t = lax.axis_index("tile")
    slots = theta_ref.shape[0]
    share = theta_ref.shape[1]
    pieces = share // LANES
    grid = prop_v.shape[1]
    rows = grid // tiles
    parts = 2 * rows
    columns = grid // LANES
    groups = tiles // 4
    field_rows = 2 * slots * rows

    first = [
        pltpu.make_async_copy(dev_hbm, dev_ref, local_sem.at[0]),
        pltpu.make_async_copy(slot_hbm, slot_ref, local_sem.at[1]),
        pltpu.make_async_copy(theta_hbm, theta_ref, local_sem.at[2]),
        pltpu.make_async_copy(weight_hbm, weight_ref, local_sem.at[3]),
        pltpu.make_async_copy(coupling_hbm, coupling_ref, local_sem.at[4]),
        pltpu.make_async_copy(cellx_hbm, cellx_v, local_sem.at[5]),
        pltpu.make_async_copy(celly_hbm, celly_v, local_sem.at[6]),
        pltpu.make_async_copy(prop_hbm, prop_v, local_sem.at[7]),
    ]
    field_loads = [
        pltpu.make_async_copy(
            field_hbm.at[:, pl.ds(q * LANES, LANES)], field_v.at[q, pl.ds(0, field_rows)], local_sem.at[8 + q]
        )
        for q in range(columns)
    ]
    for load in first + field_loads:
        load.start()
    barrier = pltpu.get_barrier_semaphore()

    def greet_cut(step, carry):
        pl.semaphore_signal(barrier, inc=1, device_id=(lax.rem(c + step, cuts), t), device_id_type=MESH)
        return carry

    def greet_tile(step, carry):
        pl.semaphore_signal(barrier, inc=1, device_id=(c, lax.rem(t + step, tiles)), device_id_type=MESH)
        return carry

    lax.fori_loop(1, cuts, greet_cut, 0)
    lax.fori_loop(1, tiles, greet_tile, 0)
    pl.semaphore_signal(
        barrier, inc=1, device_id=(lax.rem(c + cuts - 1, cuts), tiles - 1), device_id_type=MESH
    )

    first[0].wait()
    first[1].wait()
    rank_tables(c, dev_ref[...], slot_ref[...], cuts, tables_v)
    to_scalar = pltpu.make_async_copy(tables_v, tables_s, local_sem.at[11])
    to_scalar.start()

    first[2].wait()
    turns = theta_ref[...] * (HARM / (2.0 * math.pi))
    turns = turns - jnp.floor(turns + 0.5)
    turns = jnp.minimum(jnp.floor(turns * 65536.0 + 0.5), 32767.0)
    for piece in range(pieces):
        phase_v[:, piece, :] = turns[:, piece * LANES : (piece + 1) * LANES]
    def hop_copy(which, src, dst):
        return pltpu.make_async_remote_copy(
            src_ref=src,
            dst_ref=dst,
            send_sem=hop_ss.at[which],
            recv_sem=hop_rs.at[which],
            device_id=(lax.rem(c + 1, cuts), t),
            device_id_type=MESH,
        )

    def block_copy(src, dst, to, send, recv):
        return pltpu.make_async_remote_copy(
            src_ref=src, dst_ref=dst, send_sem=send, recv_sem=recv, device_id=(c, to), device_id_type=MESH
        )

    def deliver(src, dst, to, send, recv, place=t):
        @pl.when(to == t)
        def _():
            pltpu.make_async_copy(src, dst.at[place], recv.at[place]).start()

        @pl.when(to != t)
        def _():
            block_copy(src, dst.at[place], to, send.at[to], recv.at[place]).start()

    def arrive(dst, other, recv):
        block_copy(back_send.at[0], dst.at[other], other, back_ss.at[0], recv.at[other]).wait_recv()

    def stage_field(slot):
        pieces_re = [field_v[q, pl.ds(slot, rows, stride=2 * slots), :] for q in range(columns)]
        pieces_im = [field_v[q, pl.ds(slot + slots, rows, stride=2 * slots), :] for q in range(columns)]
        field_send[slot] = jnp.concatenate(
            [jnp.concatenate(pieces_re, 1), jnp.concatenate(pieces_im, 1)], 0
        ).astype(BF16)

    for load in field_loads:
        load.wait()
    stage_field(slots - 1)
    pl.semaphore_wait(barrier, cuts + tiles - 2 + tiles * (t // (tiles - 1)))
    hop_copy(0, field_send.at[slots - 1], field_hop.at[0]).start()
    to_scalar.wait()

    def pick(block, carry):
        for rank in range(CAP):
            chosen = jnp.clip(tables_s[8 + rank, block], 0, slots - 1)
            outgoing[block * CAP + rank] = phase_v[chosen].astype(jnp.int32).astype(jnp.int16)
        return carry

    lax.fori_loop(0, cuts, pick, 0)

    def theta_copy(to, slot_of, sem_of):
        return pltpu.make_async_remote_copy(
            src_ref=outgoing.at[pl.ds(to * CAP, CAP)],
            dst_ref=arrived.at[pl.ds(slot_of * CAP, CAP)],
            send_sem=theta_ss.at[to],
            recv_sem=theta_rs.at[sem_of],
            device_id=(to, t),
            device_id_type=MESH,
        )

    def theta_start(step, carry):
        theta_copy(lax.rem(c + step, cuts), c, c).start()
        return carry

    lax.fori_loop(1, cuts, theta_start, 0)
    own_theta = pltpu.make_async_copy(
        outgoing.at[pl.ds(c * CAP, CAP)], arrived.at[pl.ds(c * CAP, CAP)], theta_rs.at[c]
    )
    own_theta.start()

    def one_field(step, carry):
        slot = lax.rem(t + turn(step, slots), slots)

        @pl.when(slot < slots - 1)
        def _():
            stage_field(slot)
            deliver(field_send.at[slot], field_recv, slot + 1, field_ss, field_rs)

        return carry

    lax.fori_loop(0, slots, one_field, 0)
    hop_copy(0, field_send.at[0], field_hop.at[0]).wait_recv()
    deliver(field_hop.at[0], field_recv, 0, field_ss, field_rs)

    for load in first[3:]:
        load.wait()

    def codes(index, carry):
        cell_x = cellx_v[index]
        cell_y = celly_v[index]
        code = (cell_y // LANES) * rows + cell_x
        column = cell_y % LANES
        for k in range(2):
            row_code[2 * index + k] = jnp.broadcast_to(code[k : k + 1].astype(F32), (16, share)).astype(BF16)
            col_code[2 * index + k] = jnp.broadcast_to(column[k : k + 1].astype(F32), (16, share)).astype(BF16)
        return carry

    lax.fori_loop(0, slots, codes, 0)
    full[0:grid, 0:grid] = prop_v[0]
    full[0:grid, grid:] = -prop_v[1]
    full[grid:, 0:grid] = prop_v[1]
    full[grid:, grid:] = prop_v[0]

    own_theta.wait()

    def theta_end(step, carry):
        other = lax.rem(c + step, cuts)
        theta_copy(other, other, other).wait_recv()
        return carry

    lax.fori_loop(1, cuts, theta_end, 0)

    width = 4 * LANES
    subs = lax.broadcasted_iota(jnp.int32, (16, width), 0)
    levels = [(subs + 16 * level).astype(F32).astype(BF16) for level in range(8)]
    one = jnp.ones((16, width), BF16)
    zero = jnp.zeros((16, width), BF16)
    c0r, c0i = coupling_ref[0, 0], coupling_ref[0, 1]
    c1r, c1i = coupling_ref[1, 0], coupling_ref[1, 1]

    def deposit(slot):
        total = None
        for k in range(2):
            entry = c * slots + slot
            row = jnp.clip(tables_s[k, entry], 0, cuts * CAP - 1)
            weight = weight_ref[k, entry]
            phase = arrived[row].astype(jnp.int32).astype(F32) * (1.0 / 32768.0)
            cosine = sin_pi(0.5 - jnp.abs(phase))
            sine = sin_pi(jnp.maximum(jnp.minimum(phase, 1.0 - phase), -1.0 - phase))
            value_re = weight * cosine
            value_im = weight * sine
            index = 2 * slot + k
            for group in range(pieces // 4):
                lanes = slice(group * width, (group + 1) * width)
                column = col_code[index, :, lanes]
                code = row_code[index, :, lanes]
                spread_re = jnp.concatenate(
                    [jnp.broadcast_to(value_re[4 * group + i : 4 * group + i + 1], (16, LANES)) for i in range(4)], 1
                ).astype(BF16)
                spread_im = jnp.concatenate(
                    [jnp.broadcast_to(value_im[4 * group + i : 4 * group + i + 1], (16, LANES)) for i in range(4)], 1
                ).astype(BF16)
                hits = [code == level for level in levels[:5]]
                left = jnp.concatenate(
                    [jnp.where(hit, spread_re, zero) for hit in hits]
                    + [jnp.where(hit, spread_im, zero) for hit in hits],
                    0,
                )
                right = jnp.concatenate([jnp.where(column == level, one, zero) for level in levels], 0)
                product = dot_nt(left, right)
                total = product if total is None else total + product
        real_part = jnp.concatenate([total[i * rows : (i + 1) * rows] for i in range(3)], 1)
        imag_part = jnp.concatenate([total[80 + i * rows : 80 + (i + 1) * rows] for i in range(3)], 1)
        source_send[slot] = jnp.concatenate([real_part, imag_part], 0).astype(BF16)

    deposit(slots - 1)
    hop_copy(1, source_send.at[slots - 1], source_hop.at[0]).start()
    deliver(source_send.at[slots - 1], near_recv, slots - 1, near_ss, near_rs)

    def one_slot(step, carry):
        slot = lax.rem(t + turn(step, slots), slots)

        @pl.when(slot < slots - 1)
        def _():
            deposit(slot)
            deliver(source_send.at[slot], far_recv, slot + 1, far_ss, far_rs)

        @pl.when((lax.rem(slot, 2) == 1) & (slot < slots - 1))
        def _():
            deliver(source_send.at[slot], near_recv, slot, near_ss, near_rs)

        @pl.when(step == 12)
        def _():
            hop_copy(1, source_send.at[0], source_hop.at[0]).wait_recv()
            deliver(source_hop.at[0], far_recv, 0, far_ss, far_rs)

        return carry

    lax.fori_loop(0, slots, one_slot, 0)

    def field_in(other, carry):
        arrive(field_recv, other, field_rs)
        return carry

    lax.fori_loop(0, tiles, field_in, 0)
    odd = lax.rem(t, 2) == 1

    def pair_of(ref, pair):
        first = ref[2 * pair].astype(F32)
        second = ref[2 * pair + 1].astype(F32)
        real_part = jnp.concatenate([first[:rows], second[:rows]], 0)
        imag_part = jnp.concatenate([first[rows:], second[rows:]], 0)
        return real_part, imag_part

    def first_period(step, carry):
        group = lax.rem(t // 4 + turn(step, groups), groups)
        for i in range(4):
            other = 4 * group + i
            arrive(far_recv, other, far_rs)

            @pl.when(odd)
            def _():
                block_copy(
                    far_recv.at[other], near_recv.at[other], t - 1, twin_ss.at[other], near_rs.at[other]
                ).start()

        blocks = []
        for i in range(2):
            field_re, field_im = pair_of(field_recv, 2 * group + i)
            source_re, source_im = pair_of(far_recv, 2 * group + i)
            sum_re = field_re + c0r * source_re - c0i * source_im
            sum_im = field_im + c0r * source_im + c0i * source_re
            blocks.append(jnp.concatenate([sum_re.astype(BF16), sum_im.astype(BF16)], 1))
        inter = dot_nt(jnp.concatenate(blocks, 0), full[...])
        start = pl.multiple_of(group * 4 * rows, 4 * rows)
        tall[pl.ds(start, 4 * rows), :] = inter[:, 0:grid].astype(BF16)
        tall[pl.ds(grid + start, 4 * rows), :] = inter[:, grid:].astype(BF16)
        return carry

    lax.fori_loop(0, groups, first_period, 0)
    diff[...] = dot_nn(full[...], tall[...])

    def near_in(other, carry):
        arrive(near_recv, other, near_rs)
        return carry

    lax.fori_loop(0, tiles, near_in, 0)
    for pair in range(tiles // 2):
        real_part, imag_part = pair_of(near_recv, pair)
        top = slice(pair * parts, (pair + 1) * parts)
        low = slice(grid + pair * parts, grid + (pair + 1) * parts)
        tall[top, :] = (diff[top, :] + c1r * real_part - c1i * imag_part).astype(BF16)
        tall[low, :] = (diff[low, :] + c1r * imag_part + c1i * real_part).astype(BF16)

    def chunk_out(step, carry):
        chunk = lax.rem(t // 4 + turn(step, groups), groups)
        start = pl.multiple_of(chunk * 4 * rows, 4 * rows)
        inter_re = dot_nn(full[pl.ds(start, 4 * rows), :], tall[...])
        inter_im = dot_nn(full[pl.ds(start + grid, 4 * rows), :], tall[...])
        for i in range(4):
            to = 4 * chunk + i
            back_send[to] = jnp.concatenate(
                [inter_re[i * rows : (i + 1) * rows], inter_im[i * rows : (i + 1) * rows]], 0
            ).astype(BF16)

            @pl.when(t < tiles - 1)
            def _():
                deliver(back_send.at[to], back_recv, to, back_ss, back_rs, t + 1)

            @pl.when(t == tiles - 1)
            def _():
                pltpu.make_async_remote_copy(
                    src_ref=back_send.at[to],
                    dst_ref=back_recv.at[0],
                    send_sem=back_ss.at[to],
                    recv_sem=back_rs.at[0],
                    device_id=(lax.rem(c + 1, cuts), to),
                    device_id_type=MESH,
                ).start()

        return carry

    lax.fori_loop(0, groups, chunk_out, 0)

    def sent_theta(step, carry):
        other = lax.rem(c + step, cuts)
        theta_copy(other, other, other).wait_send()
        return carry

    lax.fori_loop(1, cuts, sent_theta, 0)

    def leave(to, send):
        block_copy(back_send.at[0], back_recv.at[0], to, send.at[to], back_rs.at[0]).wait_send()

    def sent(step, carry):
        other = lax.rem(t + step, tiles)
        leave(other, field_ss)
        leave(other, far_ss)

        @pl.when(lax.rem(other, 2) == 1)
        def _():
            leave(other, near_ss)

        return carry

    lax.fori_loop(1, tiles, sent, 0)

    @pl.when(odd)
    def _():
        def sent_twin(other, carry):
            leave(other, twin_ss)
            return carry

        lax.fori_loop(0, tiles, sent_twin, 0)

    hop_copy(0, field_send.at[0], field_hop.at[0]).wait_send()
    hop_copy(1, source_send.at[0], source_hop.at[0]).wait_send()

    def gather(step, carry):
        group = lax.rem(t // 4 + turn(step, groups), groups)
        for i in range(4):
            slot = 4 * group + i
            arrive(back_recv, slot, back_rs)
            block = back_recv[slot].astype(F32)
            for q in range(columns):
                for part in range(2):
                    field_v[q, pl.ds(part * grid + slot, rows, stride=slots), :] = block[
                        part * rows : (part + 1) * rows, q * LANES : (q + 1) * LANES
                    ]
        return carry

    lax.fori_loop(0, groups, gather, 0)
    for q in range(columns):
        for part in range(2):
            at = part * grid + q * LANES
            wide_ref[:, at : at + LANES] = field_v[q, part * grid : (part + 1) * grid, :].astype(BF16)

    def sent_back(step, carry):
        leave(lax.rem(t + step, tiles), back_ss)
        return carry

    lax.fori_loop(1, tiles, sent_back, 0)

    @pl.when(t == tiles - 1)
    def _():
        leave(t, back_ss)


def final_kernel(wide_ref, prop_ref, out_hbm, whole, sems):
    grid = prop_ref.shape[1]
    rows, _, slots, _ = whole.shape
    rows = rows // 2
    stores = []
    for i in range(2):
        real_part = wide_ref[i * rows * slots : (i + 1) * rows * slots, 0:grid]
        imag_part = wide_ref[i * rows * slots : (i + 1) * rows * slots, grid:]
        here = slice(i * rows, (i + 1) * rows)
        out_re = dot_nt(real_part, prop_ref[0]) - dot_nt(imag_part, prop_ref[1])
        whole[here, 0] = out_re.reshape(rows, slots, grid)
        out_im = dot_nt(imag_part, prop_ref[0]) + dot_nt(real_part, prop_ref[1])
        whole[here, 1] = out_im.reshape(rows, slots, grid)
        store = pltpu.make_async_copy(
            whole.at[pl.ds(i * rows, rows)], out_hbm.at[pl.ds(i * rows, rows)], sems.at[i]
        )
        store.start()
        stores.append(store)
    for store in stores:
        store.wait()


def on_device(cuts, tiles, field_in, propagator, theta, cell_x, cell_y, src_dev, src_slot, weights, coupling):
    grid = propagator.shape[1]
    rows = grid // tiles
    slots, share = theta.shape
    slices = src_dev.shape[0]
    hbm = pl.BlockSpec(memory_space=pltpu.HBM)
    vmem = pl.BlockSpec(memory_space=pltpu.VMEM)
    block = (2 * rows, grid)
    blocks = pltpu.VMEM((tiles,) + block, BF16)
    dma = pltpu.SemaphoreType.DMA
    operands = (
        theta,
        src_dev.T,
        src_slot.T,
        weights.T,
        coupling,
        field_in.reshape(rows * 2 * slots, grid),
        propagator,
        cell_x,
        cell_y,
    )
    operands = [pltpu.with_memory_space_constraint(value, pltpu.HBM) for value in operands]
    wide, prop = pl.pallas_call(
        functools.partial(section_kernel, cuts, tiles),
        out_shape=[pltpu.VMEM((grid, 2 * grid), BF16), pltpu.VMEM((2, grid, grid), BF16)],
        in_specs=[hbm] * 9,
        out_specs=[vmem, vmem],
        scratch_shapes=[
            pltpu.VMEM((slots, share), F32),
            pltpu.VMEM((2, slices), jnp.int32),
            pltpu.VMEM((2, slices), jnp.int32),
            pltpu.SMEM((2, slices), F32),
            pltpu.SMEM((2, 2), F32),
            pltpu.VMEM((grid // LANES, (rows + 1) * 2 * slots, LANES), F32),
            pltpu.VMEM((slots, 2, share), jnp.int32),
            pltpu.VMEM((slots, 2, share), jnp.int32),
            pltpu.VMEM((16, slices), jnp.int32),
            pltpu.SMEM((16, slices), jnp.int32),
            pltpu.VMEM((slots, share // LANES, LANES), F32),
            pltpu.VMEM((cuts * CAP, share // LANES, LANES), jnp.int16),
            pltpu.VMEM((cuts * CAP, share // LANES, LANES), jnp.int16),
            pltpu.VMEM((2 * slots, 16, share), BF16),
            pltpu.VMEM((2 * slots, 16, share), BF16),
            pltpu.VMEM((2 * grid, 2 * grid), BF16),
            blocks,
            blocks,
            pltpu.VMEM((1,) + block, BF16),
            pltpu.VMEM((1,) + block, BF16),
            blocks,
            blocks,
            blocks,
            pltpu.VMEM((2 * grid, grid), BF16),
            pltpu.VMEM((2 * grid, grid), F32),
            blocks,
            blocks,
            dma((12,)),
            dma((cuts,)),
            dma((cuts,)),
            dma((tiles,)),
            dma((tiles,)),
            dma((tiles,)),
            dma((tiles,)),
            dma((tiles,)),
            dma((tiles,)),
            dma((tiles,)),
            dma((2,)),
            dma((2,)),
            dma((tiles,)),
            dma((tiles,)),
        ],
        compiler_params=pltpu.CompilerParams(
            collective_id=0, has_side_effects=True, vmem_limit_bytes=48 * 1024 * 1024
        ),
    )(*operands)
    return pl.pallas_call(
        final_kernel,
        out_shape=jax.ShapeDtypeStruct((rows, 2, slots, grid), F32),
        in_specs=[vmem, vmem],
        out_specs=hbm,
        scratch_shapes=[pltpu.VMEM((rows, 2, slots, grid), F32), dma((2,))],
        compiler_params=pltpu.CompilerParams(vmem_limit_bytes=32 * 1024 * 1024),
    )(wide, prop)


def solution(mesh):
    in_specs = (
        P("tile", None, "cuts", None),
        P(),
        P("cuts", "tile"),
        P("cuts", None, "tile"),
        P("cuts", None, "tile"),
        P(),
        P(),
        P(),
        P(),
    )
    out_specs = P("tile", None, "cuts", None)
    run = functools.partial(on_device, mesh.shape["cuts"], mesh.shape["tile"])
    return jax.shard_map(run, mesh=mesh, in_specs=in_specs, out_specs=out_specs, check_vma=False)
```

```python
import functools
import math

import jax
import jax.numpy as jnp
from jax import lax
from jax.experimental import pallas as pl
from jax.experimental.pallas import tpu as pltpu
from jax.sharding import PartitionSpec as P

HARM = 5
CAP = 4
NEAR_LAG = 5
LANES = 128
MESH = pl.DeviceIdType.MESH
SIN_PI = (
    3.141592502593994,
    -5.1677069664001465,
    2.5500311851501465,
    -0.5980440974235535,
    0.07721816748380661,
)
F32 = jnp.float32
BF16 = jnp.bfloat16


def sin_pi(fraction):
    square = fraction * fraction
    total = jnp.full_like(square, SIN_PI[4])
    for coefficient in SIN_PI[3::-1]:
        total = total * square + coefficient
    return total * fraction


def turn(step, count):
    return count // 2 + (1 - 2 * lax.rem(step, 2)) * ((step + 1) // 2)


def dot_nn(left, right):
    return lax.dot_general(left, right, (((1,), (0,)), ((), ())), preferred_element_type=F32)


def dot_nt(left, right):
    return lax.dot_general(left, right, (((1,), (1,)), ((), ())), preferred_element_type=F32)


def rank_tables(me, dev, slot, cuts, tables):
    slices = dev.shape[1]
    per_block = slices // cuts
    source = lax.broadcasted_iota(jnp.int32, (cuts, slices), 0)
    low = lax.broadcasted_iota(jnp.int32, (slices, slices), 0)
    high = lax.broadcasted_iota(jnp.int32, (slices, slices), 1)
    same = low // per_block == high // per_block
    block = jnp.where(same, 1.0, 0.0).astype(BF16)
    before = jnp.where(same & (low < high), 1.0, 0.0).astype(BF16)
    hit0 = jnp.where(dev[0:1] == source, 1.0, 0.0)
    hit1 = jnp.where(dev[1:2] == source, 1.0, 0.0)
    rank0 = dot_nn(hit0.astype(BF16), before)
    rank1 = dot_nn(hit1.astype(BF16), before) + dot_nn(hit0.astype(BF16), block)
    rank0 = jnp.sum(hit0 * rank0, axis=0, keepdims=True)
    rank1 = jnp.sum(hit1 * rank1, axis=0, keepdims=True)
    arrival0 = dev[0:1] * CAP + rank0.astype(jnp.int32)
    arrival1 = dev[1:2] * CAP + rank1.astype(jnp.int32)
    tables[0:1, :] = arrival0
    tables[1:2, :] = arrival1
    wanted = lax.broadcasted_iota(jnp.int32, (8, slices), 0).astype(F32)
    mine0 = (dev[0:1] == me) & (rank0 == wanted)
    mine1 = (dev[1:2] == me) & (rank1 == wanted)
    slots = jnp.where(mine0, slot[0:1].astype(F32), 0.0) + jnp.where(mine1, slot[1:2].astype(F32), 0.0)
    place = lax.broadcasted_iota(jnp.int32, (slices, LANES), 0) // per_block
    column = lax.broadcasted_iota(jnp.int32, (slices, LANES), 1)
    chosen = dot_nn(slots.astype(BF16), jnp.where(place == column, 1.0, 0.0).astype(BF16))
    tables[8:16, 0:LANES] = chosen.astype(jnp.int32)


def section_kernel(
    cuts,
    tiles,
    theta_hbm,
    dev_hbm,
    slot_hbm,
    weight_hbm,
    coupling_hbm,
    field_hbm,
    prop_hbm,
    cellx_hbm,
    celly_hbm,
    wide_ref,
    prop_v,
    theta_ref,
    dev_ref,
    slot_ref,
    weight_ref,
    coupling_ref,
    field_v,
    cellx_v,
    celly_v,
    tables_v,
    tables_s,
    phase_v,
    outgoing,
    arrived,
    row_code,
    col_code,
    full,
    field_send,
    source_send,
    field_hop,
    source_hop,
    field_recv,
    near_recv,
    far_recv,
    tall,
    diff,
    back_send,
    back_recv,
    local_sem,
    theta_ss,
    theta_rs,
    field_ss,
    field_rs,
    near_ss,
    near_rs,
    far_ss,
    far_rs,
    twin_ss,
    hop_ss,
    hop_rs,
    back_ss,
    back_rs,
):
    c = lax.axis_index("cuts")
    t = lax.axis_index("tile")
    slots = theta_ref.shape[0]
    share = theta_ref.shape[1]
    pieces = share // LANES
    grid = prop_v.shape[1]
    rows = grid // tiles
    parts = 2 * rows
    columns = grid // LANES
    groups = tiles // 4
    field_rows = 2 * slots * rows

    first = [
        pltpu.make_async_copy(dev_hbm, dev_ref, local_sem.at[0]),
        pltpu.make_async_copy(slot_hbm, slot_ref, local_sem.at[1]),
        pltpu.make_async_copy(theta_hbm, theta_ref, local_sem.at[2]),
        pltpu.make_async_copy(weight_hbm, weight_ref, local_sem.at[3]),
        pltpu.make_async_copy(coupling_hbm, coupling_ref, local_sem.at[4]),
        pltpu.make_async_copy(cellx_hbm, cellx_v, local_sem.at[5]),
        pltpu.make_async_copy(celly_hbm, celly_v, local_sem.at[6]),
        pltpu.make_async_copy(prop_hbm, prop_v, local_sem.at[7]),
    ]
    field_loads = [
        pltpu.make_async_copy(
            field_hbm.at[:, pl.ds(q * LANES, LANES)], field_v.at[q, pl.ds(0, field_rows)], local_sem.at[8 + q]
        )
        for q in range(columns)
    ]
    for load in first + field_loads:
        load.start()
    barrier = pltpu.get_barrier_semaphore()

    def greet_cut(step, carry):
        pl.semaphore_signal(barrier, inc=1, device_id=(lax.rem(c + step, cuts), t), device_id_type=MESH)
        return carry

    def greet_tile(step, carry):
        pl.semaphore_signal(barrier, inc=1, device_id=(c, lax.rem(t + step, tiles)), device_id_type=MESH)
        return carry

    lax.fori_loop(1, cuts, greet_cut, 0)
    lax.fori_loop(1, tiles, greet_tile, 0)
    pl.semaphore_signal(
        barrier, inc=1, device_id=(lax.rem(c + cuts - 1, cuts), tiles - 1), device_id_type=MESH
    )

    first[0].wait()
    first[1].wait()
    rank_tables(c, dev_ref[...], slot_ref[...], cuts, tables_v)
    to_scalar = pltpu.make_async_copy(tables_v, tables_s, local_sem.at[11])
    to_scalar.start()

    first[2].wait()
    turns = theta_ref[...] * (HARM / (2.0 * math.pi))
    turns = turns - jnp.floor(turns + 0.5)
    turns = jnp.minimum(jnp.floor(turns * 65536.0 + 0.5), 32767.0)
    for piece in range(pieces):
        phase_v[:, piece, :] = turns[:, piece * LANES : (piece + 1) * LANES]
    def hop_copy(which, src, dst):
        return pltpu.make_async_remote_copy(
            src_ref=src,
            dst_ref=dst,
            send_sem=hop_ss.at[which],
            recv_sem=hop_rs.at[which],
            device_id=(lax.rem(c + 1, cuts), t),
            device_id_type=MESH,
        )

    def block_copy(src, dst, to, send, recv):
        return pltpu.make_async_remote_copy(
            src_ref=src, dst_ref=dst, send_sem=send, recv_sem=recv, device_id=(c, to), device_id_type=MESH
        )

    def deliver(src, dst, to, send, recv, place=t):
        @pl.when(to == t)
        def _():
            pltpu.make_async_copy(src, dst.at[place], recv.at[place]).start()

        @pl.when(to != t)
        def _():
            block_copy(src, dst.at[place], to, send.at[to], recv.at[place]).start()

    def arrive(dst, other, recv):
        block_copy(back_send.at[0], dst.at[other], other, back_ss.at[0], recv.at[other]).wait_recv()

    def stage_field(slot):
        pieces_re = [field_v[q, pl.ds(slot, rows, stride=2 * slots), :] for q in range(columns)]
        pieces_im = [field_v[q, pl.ds(slot + slots, rows, stride=2 * slots), :] for q in range(columns)]
        field_send[slot] = jnp.concatenate(
            [jnp.concatenate(pieces_re, 1), jnp.concatenate(pieces_im, 1)], 0
        ).astype(BF16)

    for load in field_loads:
        load.wait()
    stage_field(slots - 1)
    pl.semaphore_wait(barrier, cuts + tiles - 2 + tiles * (t // (tiles - 1)))
    hop_copy(0, field_send.at[slots - 1], field_hop.at[0]).start()
    to_scalar.wait()

    def pick(block, carry):
        for rank in range(CAP):
            chosen = jnp.clip(tables_s[8 + rank, block], 0, slots - 1)
            outgoing[block * CAP + rank] = phase_v[chosen].astype(jnp.int32).astype(jnp.int16)
        return carry

    lax.fori_loop(0, cuts, pick, 0)

    def theta_copy(to, slot_of, sem_of):
        return pltpu.make_async_remote_copy(
            src_ref=outgoing.at[pl.ds(to * CAP, CAP)],
            dst_ref=arrived.at[pl.ds(slot_of * CAP, CAP)],
            send_sem=theta_ss.at[to],
            recv_sem=theta_rs.at[sem_of],
            device_id=(to, t),
            device_id_type=MESH,
        )

    def theta_start(step, carry):
        theta_copy(lax.rem(c + step, cuts), c, c).start()
        return carry

    lax.fori_loop(1, cuts, theta_start, 0)
    own_theta = pltpu.make_async_copy(
        outgoing.at[pl.ds(c * CAP, CAP)], arrived.at[pl.ds(c * CAP, CAP)], theta_rs.at[c]
    )
    own_theta.start()

    def one_field(step, carry):
        slot = lax.rem(t + turn(step, slots), slots)

        @pl.when(slot < slots - 1)
        def _():
            stage_field(slot)
            deliver(field_send.at[slot], field_recv, slot + 1, field_ss, field_rs)

        return carry

    lax.fori_loop(0, slots, one_field, 0)
    hop_copy(0, field_send.at[0], field_hop.at[0]).wait_recv()
    deliver(field_hop.at[0], field_recv, 0, field_ss, field_rs)

    for load in first[3:]:
        load.wait()

    def codes(index, carry):
        cell_x = cellx_v[index]
        cell_y = celly_v[index]
        code = (cell_y // LANES) * rows + cell_x
        column = cell_y % LANES
        for k in range(2):
            row_code[2 * index + k] = jnp.broadcast_to(code[k : k + 1].astype(F32), (16, share)).astype(BF16)
            col_code[2 * index + k] = jnp.broadcast_to(column[k : k + 1].astype(F32), (16, share)).astype(BF16)
        return carry

    lax.fori_loop(0, slots, codes, 0)
    full[0:grid, 0:grid] = prop_v[0]
    full[0:grid, grid:] = -prop_v[1]
    full[grid:, 0:grid] = prop_v[1]
    full[grid:, grid:] = prop_v[0]

    own_theta.wait()

    def theta_end(step, carry):
        other = lax.rem(c + step, cuts)
        theta_copy(other, other, other).wait_recv()
        return carry

    lax.fori_loop(1, cuts, theta_end, 0)

    width = 4 * LANES
    subs = lax.broadcasted_iota(jnp.int32, (16, width), 0)
    levels = [(subs + 16 * level).astype(F32).astype(BF16) for level in range(8)]
    one = jnp.ones((16, width), BF16)
    zero = jnp.zeros((16, width), BF16)
    c0r, c0i = coupling_ref[0, 0], coupling_ref[0, 1]
    c1r, c1i = coupling_ref[1, 0], coupling_ref[1, 1]

    def deposit(slot):
        total = None
        for k in range(2):
            entry = c * slots + slot
            row = jnp.clip(tables_s[k, entry], 0, cuts * CAP - 1)
            weight = weight_ref[k, entry]
            phase = arrived[row].astype(jnp.int32).astype(F32) * (1.0 / 32768.0)
            cosine = sin_pi(0.5 - jnp.abs(phase))
            sine = sin_pi(jnp.maximum(jnp.minimum(phase, 1.0 - phase), -1.0 - phase))
            value_re = weight * cosine
            value_im = weight * sine
            index = 2 * slot + k
            for group in range(pieces // 4):
                lanes = slice(group * width, (group + 1) * width)
                column = col_code[index, :, lanes]
                code = row_code[index, :, lanes]
                spread_re = jnp.concatenate(
                    [jnp.broadcast_to(value_re[4 * group + i : 4 * group + i + 1], (16, LANES)) for i in range(4)], 1
                ).astype(BF16)
                spread_im = jnp.concatenate(
                    [jnp.broadcast_to(value_im[4 * group + i : 4 * group + i + 1], (16, LANES)) for i in range(4)], 1
                ).astype(BF16)
                hits = [code == level for level in levels[:5]]
                left = jnp.concatenate(
                    [jnp.where(hit, spread_re, zero) for hit in hits]
                    + [jnp.where(hit, spread_im, zero) for hit in hits],
                    0,
                )
                right = jnp.concatenate([jnp.where(column == level, one, zero) for level in levels], 0)
                product = dot_nt(left, right)
                total = product if total is None else total + product
        real_part = jnp.concatenate([total[i * rows : (i + 1) * rows] for i in range(3)], 1)
        imag_part = jnp.concatenate([total[80 + i * rows : 80 + (i + 1) * rows] for i in range(3)], 1)
        source_send[slot] = jnp.concatenate([real_part, imag_part], 0).astype(BF16)

    deposit(slots - 1)
    hop_copy(1, source_send.at[slots - 1], source_hop.at[0]).start()
    deliver(source_send.at[slots - 1], near_recv, slots - 1, near_ss, near_rs)

    def near_out(step, carry):
        slot = lax.rem(t + turn(step, slots), slots)

        @pl.when((lax.rem(slot, 2) == 1) & (slot < slots - 1))
        def _():
            deliver(source_send.at[slot], near_recv, slot, near_ss, near_rs)

        return carry

    def one_slot(step, carry):
        slot = lax.rem(t + turn(step, slots), slots)

        @pl.when(slot < slots - 1)
        def _():
            deposit(slot)
            deliver(source_send.at[slot], far_recv, slot + 1, far_ss, far_rs)

        @pl.when(step >= NEAR_LAG)
        def _():
            near_out(step - NEAR_LAG, 0)

        @pl.when(step == 12)
        def _():
            hop_copy(1, source_send.at[0], source_hop.at[0]).wait_recv()
            deliver(source_hop.at[0], far_recv, 0, far_ss, far_rs)

        return carry

    lax.fori_loop(0, slots, one_slot, 0)
    lax.fori_loop(slots - NEAR_LAG, slots, near_out, 0)

    def field_in(other, carry):
        arrive(field_recv, other, field_rs)
        return carry

    lax.fori_loop(0, tiles, field_in, 0)
    odd = lax.rem(t, 2) == 1

    def pair_of(ref, pair):
        first = ref[2 * pair].astype(F32)
        second = ref[2 * pair + 1].astype(F32)
        real_part = jnp.concatenate([first[:rows], second[:rows]], 0)
        imag_part = jnp.concatenate([first[rows:], second[rows:]], 0)
        return real_part, imag_part

    def first_period(step, carry):
        group = lax.rem(t // 4 + turn(step, groups), groups)
        for i in range(4):
            other = 4 * group + i
            arrive(far_recv, other, far_rs)

            @pl.when(odd)
            def _():
                block_copy(
                    far_recv.at[other], near_recv.at[other], t - 1, twin_ss.at[other], near_rs.at[other]
                ).start()

        blocks = []
        for i in range(2):
            field_re, field_im = pair_of(field_recv, 2 * group + i)
            source_re, source_im = pair_of(far_recv, 2 * group + i)
            sum_re = field_re + c0r * source_re - c0i * source_im
            sum_im = field_im + c0r * source_im + c0i * source_re
            blocks.append(jnp.concatenate([sum_re.astype(BF16), sum_im.astype(BF16)], 1))
        inter = dot_nt(jnp.concatenate(blocks, 0), full[...])
        start = pl.multiple_of(group * 4 * rows, 4 * rows)
        tall[pl.ds(start, 4 * rows), :] = inter[:, 0:grid].astype(BF16)
        tall[pl.ds(grid + start, 4 * rows), :] = inter[:, grid:].astype(BF16)
        return carry

    lax.fori_loop(0, groups, first_period, 0)
    diff[...] = dot_nn(full[...], tall[...])

    def near_in(other, carry):
        arrive(near_recv, other, near_rs)
        return carry

    lax.fori_loop(0, tiles, near_in, 0)
    for pair in range(tiles // 2):
        real_part, imag_part = pair_of(near_recv, pair)
        top = slice(pair * parts, (pair + 1) * parts)
        low = slice(grid + pair * parts, grid + (pair + 1) * parts)
        tall[top, :] = (diff[top, :] + c1r * real_part - c1i * imag_part).astype(BF16)
        tall[low, :] = (diff[low, :] + c1r * imag_part + c1i * real_part).astype(BF16)

    def chunk_out(step, carry):
        chunk = lax.rem(t // 4 + turn(step, groups), groups)
        start = pl.multiple_of(chunk * 4 * rows, 4 * rows)
        inter_re = dot_nn(full[pl.ds(start, 4 * rows), :], tall[...])
        inter_im = dot_nn(full[pl.ds(start + grid, 4 * rows), :], tall[...])
        for i in range(4):
            to = 4 * chunk + i
            back_send[to] = jnp.concatenate(
                [inter_re[i * rows : (i + 1) * rows], inter_im[i * rows : (i + 1) * rows]], 0
            ).astype(BF16)

            @pl.when(t < tiles - 1)
            def _():
                deliver(back_send.at[to], back_recv, to, back_ss, back_rs, t + 1)

            @pl.when(t == tiles - 1)
            def _():
                pltpu.make_async_remote_copy(
                    src_ref=back_send.at[to],
                    dst_ref=back_recv.at[0],
                    send_sem=back_ss.at[to],
                    recv_sem=back_rs.at[0],
                    device_id=(lax.rem(c + 1, cuts), to),
                    device_id_type=MESH,
                ).start()

        return carry

    lax.fori_loop(0, groups, chunk_out, 0)

    def sent_theta(step, carry):
        other = lax.rem(c + step, cuts)
        theta_copy(other, other, other).wait_send()
        return carry

    lax.fori_loop(1, cuts, sent_theta, 0)

    def leave(to, send):
        block_copy(back_send.at[0], back_recv.at[0], to, send.at[to], back_rs.at[0]).wait_send()

    def sent(step, carry):
        other = lax.rem(t + step, tiles)
        leave(other, field_ss)
        leave(other, far_ss)

        @pl.when(lax.rem(other, 2) == 1)
        def _():
            leave(other, near_ss)

        return carry

    lax.fori_loop(1, tiles, sent, 0)

    @pl.when(odd)
    def _():
        def sent_twin(other, carry):
            leave(other, twin_ss)
            return carry

        lax.fori_loop(0, tiles, sent_twin, 0)

    hop_copy(0, field_send.at[0], field_hop.at[0]).wait_send()
    hop_copy(1, source_send.at[0], source_hop.at[0]).wait_send()

    def gather(step, carry):
        group = lax.rem(t // 4 + turn(step, groups), groups)
        for i in range(4):
            slot = 4 * group + i
            arrive(back_recv, slot, back_rs)
            block = back_recv[slot].astype(F32)
            for q in range(columns):
                for part in range(2):
                    field_v[q, pl.ds(part * grid + slot, rows, stride=slots), :] = block[
                        part * rows : (part + 1) * rows, q * LANES : (q + 1) * LANES
                    ]
        return carry

    lax.fori_loop(0, groups, gather, 0)
    for q in range(columns):
        for part in range(2):
            at = part * grid + q * LANES
            wide_ref[:, at : at + LANES] = field_v[q, part * grid : (part + 1) * grid, :].astype(BF16)

    def sent_back(step, carry):
        leave(lax.rem(t + step, tiles), back_ss)
        return carry

    lax.fori_loop(1, tiles, sent_back, 0)

    @pl.when(t == tiles - 1)
    def _():
        leave(t, back_ss)


def final_kernel(wide_ref, prop_ref, out_hbm, whole, sems):
    grid = prop_ref.shape[1]
    rows, _, slots, _ = whole.shape
    rows = rows // 2
    stores = []
    for i in range(2):
        real_part = wide_ref[i * rows * slots : (i + 1) * rows * slots, 0:grid]
        imag_part = wide_ref[i * rows * slots : (i + 1) * rows * slots, grid:]
        here = slice(i * rows, (i + 1) * rows)
        out_re = dot_nt(real_part, prop_ref[0]) - dot_nt(imag_part, prop_ref[1])
        whole[here, 0] = out_re.reshape(rows, slots, grid)
        out_im = dot_nt(imag_part, prop_ref[0]) + dot_nt(real_part, prop_ref[1])
        whole[here, 1] = out_im.reshape(rows, slots, grid)
        store = pltpu.make_async_copy(
            whole.at[pl.ds(i * rows, rows)], out_hbm.at[pl.ds(i * rows, rows)], sems.at[i]
        )
        store.start()
        stores.append(store)
    for store in stores:
        store.wait()


def on_device(cuts, tiles, field_in, propagator, theta, cell_x, cell_y, src_dev, src_slot, weights, coupling):
    grid = propagator.shape[1]
    rows = grid // tiles
    slots, share = theta.shape
    slices = src_dev.shape[0]
    hbm = pl.BlockSpec(memory_space=pltpu.HBM)
    vmem = pl.BlockSpec(memory_space=pltpu.VMEM)
    block = (2 * rows, grid)
    blocks = pltpu.VMEM((tiles,) + block, BF16)
    dma = pltpu.SemaphoreType.DMA
    operands = (
        theta,
        src_dev.T,
        src_slot.T,
        weights.T,
        coupling,
        field_in.reshape(rows * 2 * slots, grid),
        propagator,
        cell_x,
        cell_y,
    )
    operands = [pltpu.with_memory_space_constraint(value, pltpu.HBM) for value in operands]
    wide, prop = pl.pallas_call(
        functools.partial(section_kernel, cuts, tiles),
        out_shape=[pltpu.VMEM((grid, 2 * grid), BF16), pltpu.VMEM((2, grid, grid), BF16)],
        in_specs=[hbm] * 9,
        out_specs=[vmem, vmem],
        scratch_shapes=[
            pltpu.VMEM((slots, share), F32),
            pltpu.VMEM((2, slices), jnp.int32),
            pltpu.VMEM((2, slices), jnp.int32),
            pltpu.SMEM((2, slices), F32),
            pltpu.SMEM((2, 2), F32),
            pltpu.VMEM((grid // LANES, (rows + 1) * 2 * slots, LANES), F32),
            pltpu.VMEM((slots, 2, share), jnp.int32),
            pltpu.VMEM((slots, 2, share), jnp.int32),
            pltpu.VMEM((16, slices), jnp.int32),
            pltpu.SMEM((16, slices), jnp.int32),
            pltpu.VMEM((slots, share // LANES, LANES), F32),
            pltpu.VMEM((cuts * CAP, share // LANES, LANES), jnp.int16),
            pltpu.VMEM((cuts * CAP, share // LANES, LANES), jnp.int16),
            pltpu.VMEM((2 * slots, 16, share), BF16),
            pltpu.VMEM((2 * slots, 16, share), BF16),
            pltpu.VMEM((2 * grid, 2 * grid), BF16),
            blocks,
            blocks,
            pltpu.VMEM((1,) + block, BF16),
            pltpu.VMEM((1,) + block, BF16),
            blocks,
            blocks,
            blocks,
            pltpu.VMEM((2 * grid, grid), BF16),
            pltpu.VMEM((2 * grid, grid), F32),
            blocks,
            blocks,
            dma((12,)),
            dma((cuts,)),
            dma((cuts,)),
            dma((tiles,)),
            dma((tiles,)),
            dma((tiles,)),
            dma((tiles,)),
            dma((tiles,)),
            dma((tiles,)),
            dma((tiles,)),
            dma((2,)),
            dma((2,)),
            dma((tiles,)),
            dma((tiles,)),
        ],
        compiler_params=pltpu.CompilerParams(
            collective_id=0, has_side_effects=True, vmem_limit_bytes=48 * 1024 * 1024
        ),
    )(*operands)
    return pl.pallas_call(
        final_kernel,
        out_shape=jax.ShapeDtypeStruct((rows, 2, slots, grid), F32),
        in_specs=[vmem, vmem],
        out_specs=hbm,
        scratch_shapes=[pltpu.VMEM((rows, 2, slots, grid), F32), dma((2,))],
        compiler_params=pltpu.CompilerParams(vmem_limit_bytes=32 * 1024 * 1024),
    )(wide, prop)


def solution(mesh):
    in_specs = (
        P("tile", None, "cuts", None),
        P(),
        P("cuts", "tile"),
        P("cuts", None, "tile"),
        P("cuts", None, "tile"),
        P(),
        P(),
        P(),
        P(),
    )
    out_specs = P("tile", None, "cuts", None)
    run = functools.partial(on_device, mesh.shape["cuts"], mesh.shape["tile"])
    return jax.shard_map(run, mesh=mesh, in_specs=in_specs, out_specs=out_specs, check_vma=False)
```
